512 devices in a mesh: pipe: 4 (over y), ctx: 32 (over z, core), tp: 4 (over x).
Axes of the slice: x: 4, y: 4, z: 16, core: 2. Of those that a mesh axis runs over, the one named last changes fastest.
Arguments:
- hidden_in: bfloat16 [4, 4096, 4096], P('pipe', 'ctx', 'tp'), may hold values from -8 to 8
- doc_ids: int32 [4096], P('ctx'), may hold values from 0 to 3, never falling along the last dimension, each value on 1 to 2048 neighbouring positions
- layer_kind: int32 [4], P('pipe'), may hold values from 0 to 1, as said below
- norm_gain: float32 [4, 4096], P('pipe', 'tp'), may hold values from 0.5 to 1.5
- q_weight: bfloat16 [4, 4096, 4096], P('pipe', 'ctx', 'tp'), may hold values from -2 to 2
- k_weight: bfloat16 [4, 4096, 512], P('pipe', 'ctx', 'tp'), may hold values from -1 to 1
- v_weight: bfloat16 [4, 4096, 512], P('pipe', 'ctx', 'tp'), may hold values from -0.09375 to 0.09375
- bc_weight: bfloat16 [4, 4096, 32], P('pipe', 'tp'), may hold values from -0.046875 to 0.046875
- dt_weight: bfloat16 [4, 4096, 64], P('pipe', 'tp'), may hold values from -0.09375 to 0.09375
- dt_bias: float32 [4, 64], P('pipe', 'tp'), may hold values from -1 to 1
- decay_rate: float32 [4, 64], P('pipe', 'tp'), may hold values from 1.2207031e-05 to 0.05
- skip_gain: float32 [4, 64], P('pipe', 'tp'), may hold values from 0.5 to 1.5
Outputs:
- section_out: bfloat16 [4, 4096, 4096], P('pipe', 'ctx', 'tp')
- passed: bfloat16 [4, 4096, 4096], P('pipe', 'ctx', 'tp')
The draws below stay inside these ranges and needn't reach their ends.
Inputs may be any that keep to these rules, and one draw needn't show every extreme that they name: `layer_kind`: every draw has at least one attention section and at least one state-space section.
All inputs are finite; a program needn't handle non-finite values.
Results may differ from the reference program's by a relative error of at most 0.011.
Values may be sent and summed in bfloat16 or wider, within the bound.
No kernel may reach another device: no remote copies, remote signals or barrier semaphores. Data moves between devices by JAX's collectives and lax.ppermute only.
A program may use at most 64 MiB of HBM per device.

```python
import math
import jax
import jax.numpy as jnp
import numpy as np
from jax import lax

D = 4096
HEADS = 32
KVH = 4
HD = 128
STATE = 16
SSM_P = 64
SEQ = 4096
SECTIONS = 4
SSM_HEADS = 64


def draw_layer_kind(key, part):
    base = jnp.array([0, 1], jnp.int32)
    extra = jax.random.randint(jax.random.fold_in(key, 11), (SECTIONS - 2,), 0, 2).astype(jnp.int32)
    full = jnp.concatenate([base, extra])
    return jax.random.permutation(jax.random.fold_in(key, 12), full).astype(jnp.int32)


def draw_hidden_in(key, part):
    drawn = jnp.clip(jax.random.normal(jax.random.fold_in(key, 31), (SECTIONS, SEQ, D), jnp.float32), -6.0, 6.0)
    return drawn.astype(jnp.bfloat16)


def draw_q_weight(key, part):
    columns = HEADS * HD
    drawn = jnp.clip(jax.random.normal(jax.random.fold_in(key, 21), (SECTIONS, D, columns), jnp.float32), -6.0, 6.0) * (3.0 * D ** (-0.5))
    return drawn.astype(jnp.bfloat16)


def draw_k_weight(key, part):
    columns = KVH * HD
    drawn = jnp.clip(jax.random.normal(jax.random.fold_in(key, 22), (SECTIONS, D, columns), jnp.float32), -6.0, 6.0) * D ** (-0.5)
    return drawn.astype(jnp.bfloat16)


def block_scale(own_key, shape, shards, least, largest):
    def one(axis_at, blocks):
        steps = jax.random.uniform(jax.random.fold_in(jax.random.fold_in(own_key, 6), axis_at), (blocks,), jnp.float32, least / len(shards), largest / len(shards))
        return jnp.repeat(jnp.exp(steps), shape[axis_at] // blocks).reshape((-1,) + (1,) * (len(shape) - axis_at - 1))

    level = one(*shards[0])
    for cut in shards[1:]:
        level = level * one(*cut)
    return level


def split_up(number_of, total, reach, skew):
    weights = [(1 << 20) // math.isqrt(grade ** skew) + 1 for grade in range(2, number_of + 1)]
    spare, given = total - reach - (number_of - 1), [1] * (number_of - 1)
    while spare > 0:
        movable = [i for i in range(number_of - 1) if given[i] < reach]
        mass, remaining = sum([weights[i] for i in movable]), spare
        for i in movable:
            more = min(reach - given[i], max(1, remaining * weights[i] // mass), spare)
            given[i] = given[i] + more
            spare = spare - more
    return np.array([reach] + given)


def ragged(key, count, total, reach, lean):
    if count == 2:
        one = jax.random.randint(key, (), max(1, total - reach), min(reach, total - 1) + 1)
        return jnp.stack([one, total - one])
    tallies = jnp.asarray(split_up(count, total, reach, lean), jnp.int32)
    pairs = (count - 1) // 2
    donor, receiver = tallies[1:1 + 2 * pairs:2], tallies[2:2 + 2 * pairs:2]
    room = jnp.minimum(donor - 1, reach - receiver)
    shifted = jax.random.randint(jax.random.fold_in(key, 1), (pairs,), 0, 1 << 20) % (room + 1)
    tallies = tallies.at[1:1 + 2 * pairs:2].set(donor - shifted).at[2:2 + 2 * pairs:2].set(receiver + shifted)
    return tallies[jax.random.permutation(jax.random.fold_in(key, 2), count)]


def normal_values(key, extent, width, most, cuts=(), kind=jnp.bfloat16):
    values = width * jax.random.normal(key, extent, jnp.float32)
    if cuts:
        values = values * block_scale(key, extent, cuts, -0.22, 0.18)
    return jnp.clip(values, -most, most).astype(kind)


def setup_inputs(seed: int = 0) -> dict:
    splits = jax.random.split(jax.random.key(seed), 13)
    hidden_in = draw_hidden_in(jax.random.fold_in(splits[12], 71), 0)
    doc_ids = jnp.searchsorted(jnp.cumsum(ragged(splits[1], 4, SEQ, SEQ // 2, 1)), jnp.arange(SEQ), side="right").astype(jnp.int32)
    layer_kind = draw_layer_kind(jax.random.fold_in(splits[12], 71), 0)
    norm_gain = jnp.clip(1.0 + 0.1 * jax.random.normal(splits[3], (SECTIONS, D), jnp.float32), 0.5, 1.5)
    q_weight = draw_q_weight(jax.random.fold_in(splits[12], 71), 0)
    k_weight = draw_k_weight(jax.random.fold_in(splits[12], 71), 0)
    v_weight = normal_values(splits[6], (SECTIONS, D, KVH * HD), D ** -0.5, 0.09375, ((0, 4), (1, 32), (2, 4)))
    bc_weight = normal_values(splits[7], (SECTIONS, D, 2 * STATE), (4 * D) ** -0.5, 0.046875, ((0, 4), (1, 4)))
    dt_weight = normal_values(splits[8], (SECTIONS, D, SSM_HEADS), D ** -0.5, 0.09375, ((0, 4), (1, 4)))
    dt_bias = jnp.clip(jax.random.uniform(splits[9], (SECTIONS, SSM_HEADS), jnp.float32, -1.0, 1.0) * block_scale(splits[9], (SECTIONS, SSM_HEADS), ((0, 4), (1, 4)), -0.4, 0.0), -1.0, 1.0)
    decay_rate = jnp.clip(jnp.exp(math.log(0.05) - 8.317766 * jax.random.uniform(splits[10], (SECTIONS, SSM_HEADS), jnp.float32) ** block_scale(splits[10], (SECTIONS, SSM_HEADS), ((0, 4), (1, 4)), -0.2, 0.2)), 1.220703143189894e-05, 0.05)
    skip_gain = jnp.clip(0.5 + 1.0 * jax.random.uniform(splits[11], (SECTIONS, SSM_HEADS), jnp.float32) ** block_scale(splits[11], (SECTIONS, SSM_HEADS), ((0, 4), (1, 4)), -0.2, 0.2), 0.5, 1.5)
    return dict(hidden_in=hidden_in, doc_ids=doc_ids, layer_kind=layer_kind, norm_gain=norm_gain, q_weight=q_weight, k_weight=k_weight, v_weight=v_weight, bc_weight=bc_weight, dt_weight=dt_weight, dt_bias=dt_bias, decay_rate=decay_rate, skip_gain=skip_gain)


def normed(h, gain):
    hf = h.astype(jnp.float32)
    mean_sq = lax.optimization_barrier(jnp.mean(hf * hf, axis=1, keepdims=True))
    return (hf * lax.rsqrt(mean_sq + 1e-05) * gain[None, :]).astype(jnp.bfloat16)

def attention_layer(h, xn, wq, wk, wv, doc_ids):
    group = HEADS // KVH
    query = jnp.dot(xn, wq, preferred_element_type=jnp.float32).astype(jnp.bfloat16)
    query = jnp.transpose(query.reshape(SEQ, HEADS, HD), (1, 0, 2))
    keys = jnp.dot(xn, wk, preferred_element_type=jnp.float32).astype(jnp.bfloat16)
    keys = jnp.transpose(keys.reshape(SEQ, KVH, HD), (1, 0, 2))
    values = jnp.dot(xn, wv, preferred_element_type=jnp.float32).astype(jnp.bfloat16)
    values = jnp.transpose(values.reshape(SEQ, KVH, HD), (1, 0, 2))
    positions = jnp.arange(SEQ)
    block = 512 if SEQ % 512 == 0 else SEQ
    scale = HD ** (-0.5)

    def one_head(item):
        q_head, head = item
        kv_index = (head // group).astype(jnp.int32)
        k_head = lax.dynamic_index_in_dim(keys, kv_index, 0, keepdims=False)
        v_head = lax.dynamic_index_in_dim(values, kv_index, 0, keepdims=False)
        pieces = []
        for start in range(0, SEQ, block):
            end = start + block
            scores = jnp.dot(q_head[start:end], k_head[:end].T, preferred_element_type=jnp.float32) * scale
            allowed = (positions[None, :end] <= positions[start:end, None]) & (doc_ids[None, :end] == doc_ids[start:end, None])
            scores = jnp.where(allowed, scores, -jnp.inf)
            top = lax.optimization_barrier(jnp.max(scores, axis=1, keepdims=True))
            probs = jnp.where(allowed, jnp.exp(scores - top), 0.0)
            denom = lax.optimization_barrier(jnp.sum(probs, axis=1, keepdims=True))
            mixed = jnp.dot(probs.astype(jnp.bfloat16), v_head[:end], preferred_element_type=jnp.float32)
            pieces.append((mixed / denom).astype(jnp.bfloat16))
        return jnp.concatenate(pieces, axis=0)
    outputs = lax.map(one_head, (query, jnp.arange(HEADS).astype(jnp.int32)))
    attended = jnp.transpose(outputs, (1, 0, 2)).reshape(SEQ, D)
    return (h.astype(jnp.float32) + attended.astype(jnp.float32)).astype(jnp.bfloat16)

def state_layer(h, xn, wbc, wdt, bias, rate, skip, doc_ids):
    inputs = xn.astype(jnp.float32).reshape(SEQ, SSM_HEADS, SSM_P)
    step = jax.nn.softplus(jnp.dot(xn, wdt, preferred_element_type=jnp.float32) + bias[None, :])
    maps = jnp.dot(xn, wbc, preferred_element_type=jnp.float32)
    in_map = maps[:, :STATE]
    out_map = maps[:, STATE:]
    before = jnp.concatenate([jnp.full((1,), -1, jnp.int32), doc_ids[:-1].astype(jnp.int32)])
    keep = (doc_ids == before).astype(jnp.float32)
    decay = jnp.exp(-step * rate[None, :]) * keep[:, None]

    def advance(carry, item):
        dec, stp, b_row, c_row, x_row = item
        carry = dec[:, None, None] * carry + stp[:, None, None] * b_row[None, :, None] * x_row[:, None, :]
        return (carry, jnp.einsum('n,hnp->hp', c_row, carry))
    start = jnp.zeros((SSM_HEADS, STATE, SSM_P), jnp.float32)
    _, outputs = lax.scan(advance, start, (decay, step, in_map, out_map, inputs))
    outputs = outputs + skip[None, :, None] * inputs
    outputs = outputs * lax.rsqrt(lax.optimization_barrier(jnp.mean(outputs * outputs, axis=2, keepdims=True)) + 1e-05)
    return (h.astype(jnp.float32) + outputs.reshape(SEQ, D)).astype(jnp.bfloat16)

def reference(hidden_in, doc_ids, layer_kind, norm_gain, q_weight, k_weight, v_weight, bc_weight, dt_weight, dt_bias, decay_rate, skip_gain):
    results = []
    for section in range(SECTIONS):
        current = hidden_in[section]
        xn = normed(current, norm_gain[section])

        def attend_fn(h, xn=xn, section=section):
            return attention_layer(h, xn, q_weight[section], k_weight[section], v_weight[section], doc_ids)

        def state_fn(h, xn=xn, section=section):
            return state_layer(h, xn, bc_weight[section], dt_weight[section], dt_bias[section], decay_rate[section], skip_gain[section], doc_ids)
        results.append(lax.cond(layer_kind[section] == 1, attend_fn, state_fn, current))
    section_out = jnp.stack(results, axis=0)
    passed = jnp.concatenate([jnp.zeros((1, SEQ, D), jnp.bfloat16), section_out[:-1]], axis=0)
    return (section_out, passed)
```

```python
import jax
import jax.numpy as jnp
from jax import lax
from jax.experimental import pallas as pl
from jax.experimental.pallas import tpu as pltpu
from jax.sharding import PartitionSpec as P

D = 4096
HD = 128
ROWS = 128
COLS = 1024
CHIPS = 16
STATE = 16
HL = 16
PAY = ROWS + 16
BACK = 8
NEG = -1e30
BF, F32 = jnp.bfloat16, jnp.float32
EXACT = lax.Precision.HIGHEST

W_FIRST = (0, -4, 4, -8)
W_REL = tuple(a + b for b in (0, -1, 1, -2) for a in W_FIRST)
KV_AT = {0: (0, 0), 4: (0, 1), 8: (0, 2), 1: (1, 0), 5: (1, 1), 2: (1, 2), 6: (1, 3), 3: (1, 4), 7: (1, 5)}


def iota(shape, dim):
    return lax.broadcasted_iota(jnp.int32, shape, dim)


def dot(a, b, precision=None):
    return jnp.dot(a, b, preferred_element_type=F32, precision=precision)


def pair(low, j, values):
    return jnp.where(low, values[:, 2 * j : 2 * j + 1], values[:, 2 * j + 1 : 2 * j + 2])


def front(scal, got, idc_ref, idr_ref, bias, rate, skip, xn, pay, yloc, aux):
    attention, place = scal[0], scal[1]
    squares = jnp.zeros((ROWS, 1), F32)
    for s in range(4):
        hf = got[s, :ROWS, :].astype(F32)
        squares += jnp.sum(hf * hf, axis=1, keepdims=True)
    inverse = lax.rsqrt(squares / D + 1e-05)
    for s in range(4):
        gain = got[s, ROWS + 48 :, :].astype(F32)
        gain = gain[0:1] + gain[1:2] + gain[2:3]
        xn[:, s * COLS : (s + 1) * COLS] = (got[s, :ROWS, :].astype(F32) * inverse * gain).astype(BF)
    idc, idr = idc_ref[...], idr_ref[...]
    row = iota((16, 256), 0)
    ids = jnp.concatenate([idr, jnp.zeros((1, ROWS), F32)], axis=1)
    pay[ROWS:, :] = jnp.where(row == 0, ids, 0.0).astype(BF)

    @pl.when(attention == 0)
    def _():
        maps = jnp.zeros((ROWS, 48), F32)
        for s in range(4):
            maps += lax.dot_general(
                xn[:, s * COLS : (s + 1) * COLS],
                got[s, ROWS : ROWS + 48, :],
                (((1,), (1,)), ((), ())),
                preferred_element_type=F32,
            )
        raw = maps[:, :HL] + bias[...]
        step = jnp.maximum(raw, 0.0) + jnp.log1p(jnp.exp(-jnp.abs(raw)))
        in_map, out_map = maps[:, HL : HL + STATE], maps[:, HL + STATE :]
        earlier = iota((ROWS, ROWS), 0) >= iota((ROWS, ROWS), 1)
        cum = dot(earlier.astype(F32), -step * rate[...], EXACT)
        empty = jnp.zeros((ROWS, ROWS - 32), F32)
        turned = jnp.concatenate([cum, in_map, empty], axis=1).T
        cum_t, in_t = turned[:HL], turned[HL : HL + STATE]
        both = dot(out_map, in_t, EXACT)
        mask = earlier & (idc == idr)
        last = cum[ROWS - 1 :, :]
        end = jnp.where(idc == idr[:, ROWS - 1 :], jnp.exp(last - cum), 0.0)
        low = iota((ROWS, ROWS), 1) < 64
        base = pl.multiple_of(place * COLS, COLS)
        for j in range(HL // 2):
            x = xn[:, pl.ds(base + j * 128, 128)].astype(F32)
            wx = x * pair(low, j, step)
            weights = [
                jnp.exp(jnp.where(mask, cum[:, i : i + 1] - cum_t[i : i + 1, :], NEG)) * both
                for i in (2 * j, 2 * j + 1)
            ]
            split = jnp.concatenate([jnp.where(low, wx, 0.0), jnp.where(low, 0.0, wx)], axis=0)
            inner = dot(jnp.concatenate(weights, axis=1), split, EXACT)
            yloc[:, j * 128 : (j + 1) * 128] = inner + pair(low[:1], j, skip[...]) * x
            state = dot(in_t, wx * pair(low, j, end), EXACT)
            at = 16 * (j // 2)
            pay[at : at + 16, 128 * (j % 2) : 128 * (j % 2) + 128] = state.astype(BF)
        wide = jnp.concatenate([last, jnp.zeros((1, 256 - HL), F32)], axis=1)
        first = wide.astype(BF).astype(F32)
        second = (wide - first).astype(BF).astype(F32)
        third = wide - first - second
        extra = jnp.where(row == 1, first, jnp.where(row == 2, second, jnp.where(row == 3, third, 0.0)))
        pay[ROWS:, :] = jnp.where(row == 0, ids, extra).astype(BF)
        aux[...] = jnp.concatenate([cum, out_map, empty], axis=1)


def project(scal, xn, own0, own1, own2, own3, sib, state_pay, pay, weight):
    attention, chip, core = scal[0], scal[2], scal[3]

    @pl.when(attention == 1)
    def _():
        for n, rel in enumerate(W_REL):
            at = lax.rem(chip + rel + CHIPS, CHIPS) * 256
            source = (own0, own1, own2, own3)[n // 4]
            k = n % 4
            weight[pl.ds(pl.multiple_of(at + core * 128, 128), 128), :] = source[k * 128 : k * 128 + 128, :]
            weight[pl.ds(pl.multiple_of(at + (1 - core) * 128, 128), 128), :] = sib[n * 128 : n * 128 + 128, :]
        pay[:ROWS, :] = dot(xn[...], weight[...]).astype(BF)
        pay[ROWS:, :] = state_pay[ROWS:, :]

    @pl.when(attention == 0)
    def _():
        pay[...] = state_pay[...]


def attend(scal, h, xn, wq, blocks, idc_ref, out, wbuf, keys, values, mask, sem):
    chip, core = scal[2], scal[3]
    copies = [
        pltpu.make_async_copy(wq.at[:, pl.ds(j * 256, 256)], wbuf.at[j], sem.at[j]) for j in range(4)
    ]
    for copy in copies:
        copy.start()
    idc = idc_ref[...]
    n = 0
    for r in range(BACK + 1):
        which, k = KV_AT[r]
        for mine in (True, False):
            ref = blocks[which if mine else 2 + which]
            rows = slice(n * ROWS, (n + 1) * ROWS)
            keys[rows, :] = ref[k * PAY : k * PAY + ROWS, :HD]
            values[rows, :] = ref[k * PAY : k * PAY + ROWS, HD:]
            ids = ref[k * PAY + ROWS : (k + 1) * PAY, :HD].astype(F32)[0:1, :]
            allowed = idc == ids
            if r == 0 and mine:
                allowed = allowed & (iota((ROWS, ROWS), 0) >= iota((ROWS, ROWS), 1))
            else:
                valid = core == 1 if r == 0 else chip >= r
                allowed = allowed & (jnp.full((ROWS, ROWS), valid.astype(jnp.int32)) == 1)
            mask[:, rows] = jnp.where(allowed, 0.0, NEG)
            n += 1
    factor = HD ** (-0.5) * 1.4426950408889634
    for j in range(4):
        copies[j].wait()
        q = dot(xn[...], wbuf[j]).astype(BF)
        query = jnp.concatenate([q[:, :HD], q[:, HD:]], axis=0)
        scores = lax.dot_general(
            query, keys[...], (((1,), (1,)), ((), ())), preferred_element_type=F32
        )
        parts, dens = [], []
        for i in range(2):
            s = scores[i * ROWS : (i + 1) * ROWS, :] + mask[...]
            p = jnp.exp2((s - jnp.max(s, axis=1, keepdims=True)) * factor)
            dens.append(jnp.sum(p, axis=1, keepdims=True))
            parts.append(p.astype(BF))
        mixed = dot(jnp.concatenate(parts, axis=0), values[...])
        for i in range(2):
            o = (mixed[i * ROWS : (i + 1) * ROWS, :] / dens[i]).astype(BF).astype(F32)
            cols = slice(j * 256 + i * HD, j * 256 + (i + 1) * HD)
            out[:, cols] = (h[:, cols].astype(F32) + o).astype(BF)


def finish_states(scal, h, blocks, yloc, aux, idc_ref, out):
    core, device = scal[3], scal[4]
    order = []
    for r in range(1, BACK + 1):
        def block(mine, back):
            which, k = KV_AT[back]
            return blocks[which if mine else 2 + which], k * PAY

        order.append((block(False, r - 1), block(False, r)))
        order.append((block(True, r), None))

    def read(entry, lo, hi):
        (ref, at), other = entry
        tile = ref[at + lo : at + hi, :].astype(F32)
        if other is not None:
            ref, at = other
            tile = jnp.where(core == 1, tile, ref[at + lo : at + hi, :].astype(F32))
        return tile

    idc = idc_ref[...]
    before = jnp.zeros((1, HL), F32)
    coefs = []
    previous = None
    for k, entry in enumerate(order, 1):
        extra = read(entry, ROWS, PAY)
        tail = jnp.where(device >= k, extra[0:1, HD - 1 : HD], -1.0)
        if previous is None:
            previous = tail
        fits = (tail == previous) & (tail >= 0.0)
        coefs.append(jnp.where(fits, jnp.exp(before), 0.0))
        before += extra[1:2, :HL] + extra[2:3, :HL] + extra[3:4, :HL]
    spread = (iota((HL, COLS), 1) // 64 == iota((HL, COLS), 0)).astype(F32)
    coef = dot(jnp.concatenate(coefs, axis=0), spread, EXACT)
    cum, out_map = aux[:, :HL], aux[:, HL : HL + STATE]
    reach = jnp.where(idc == previous, jnp.exp(cum), 0.0)
    low = iota((ROWS, ROWS), 1) < 64
    for c in range(4):
        incoming = jnp.zeros((STATE, 256), F32)
        for k, entry in enumerate(order):
            incoming += coef[k : k + 1, c * 256 : (c + 1) * 256] * read(entry, 16 * c, 16 * c + 16)
        for i in range(2):
            j = 2 * c + i
            cols = slice(j * 128, (j + 1) * 128)
            carried = dot(out_map, incoming[:, i * 128 : (i + 1) * 128], EXACT) * pair(low, j, reach)
            y = yloc[:, cols] + carried
            y2 = y * y
            one = jnp.sum(jnp.where(low, y2, 0.0), axis=1, keepdims=True)
            two = jnp.sum(jnp.where(low, 0.0, y2), axis=1, keepdims=True)
            scale = lax.rsqrt(jnp.where(low, one, two) / 64 + 1e-05)
            out[:, cols] = (h[:, cols].astype(F32) + y * scale).astype(BF)


def finish(scal, h, xn, wq, own0, own1, sib0, sib1, yloc, aux, idc, out, wbuf, keys, values, mask, sem):
    blocks = (own0, own1, sib0, sib1)

    @pl.when(scal[0] == 1)
    def _():
        attend(scal, h, xn, wq, blocks, idc, out, wbuf, keys, values, mask, sem)

    @pl.when(scal[0] == 0)
    def _():
        finish_states(scal, h, blocks, yloc, aux, idc, out)


VMEM = pl.BlockSpec(memory_space=pltpu.VMEM)
SMEM = pl.BlockSpec(memory_space=pltpu.SMEM)
ANY = pl.BlockSpec(memory_space=pl.ANY)


def shape(*dims, dtype=BF):
    return jax.ShapeDtypeStruct(dims, dtype)


def by_chips(x, k):
    return lax.ppermute(x, "ctx", [(i, (i + 2 * k) % (2 * CHIPS)) for i in range(2 * CHIPS)])


def swap(x):
    return lax.ppermute(x, "ctx", [(i, i ^ 1) for i in range(2 * CHIPS)])


def shards(
    hidden_in,
    doc_ids,
    layer_kind,
    norm_gain,
    q_weight,
    k_weight,
    v_weight,
    bc_weight,
    dt_weight,
    dt_bias,
    decay_rate,
    skip_gain,
):
    device = lax.axis_index("ctx")
    scal = jnp.stack(
        [layer_kind[0], lax.axis_index("tp"), device // 2, device % 2, device]
    ).astype(jnp.int32)
    params = pltpu.CompilerParams(vmem_limit_bytes=48 << 20)

    wq = lax.all_gather(q_weight[0], "ctx", axis=0, tiled=True)

    wkv = jnp.concatenate([k_weight[0], v_weight[0]], axis=1)
    first = jnp.concatenate([wkv] + [by_chips(wkv, k) for k in (4, -4, 8)], axis=0)
    others = [by_chips(first, k) for k in (1, -1, 2)]
    sibling = swap(jnp.concatenate([first] + others, axis=0))

    gain = norm_gain[0]
    gain1 = lax.reduce_precision(gain, 8, 7)
    gain2 = lax.reduce_precision(gain - gain1, 8, 7)
    gain3 = gain - gain1 - gain2
    gains = jnp.concatenate([jnp.stack([gain1, gain2, gain3]), jnp.zeros((13, COLS), F32)]).astype(BF)
    everyone = lambda x: jnp.broadcast_to(x[None], (4,) + x.shape)
    got = lax.all_to_all(
        jnp.concatenate(
            [
                everyone(hidden_in[0]),
                dt_weight[0].T.reshape(4, HL, COLS),
                everyone(bc_weight[0].T),
                everyone(gains),
            ],
            axis=1,
        ),
        "tp",
        0,
        0,
    )
    ids = doc_ids.astype(F32)
    idc, idr = ids[:, None], ids[None, :]
    xn, state_pay, yloc, aux = pl.pallas_call(
        front,
        name="front",
        out_shape=(shape(ROWS, D), shape(PAY, 256), shape(ROWS, COLS, dtype=F32), shape(ROWS, 128, dtype=F32)),
        in_specs=[SMEM] + [VMEM] * 6,
        out_specs=(VMEM,) * 4,
        compiler_params=params,
        cost_estimate=pl.CostEstimate(flops=2 * 128 * 128 * 4096, bytes_accessed=4 << 20, transcendentals=0),
    )(scal, got, idc, idr, dt_bias, decay_rate, skip_gain)

    pay = pl.pallas_call(
        project,
        name="project",
        out_shape=shape(PAY, 256),
        in_specs=[SMEM] + [VMEM] * 7,
        out_specs=VMEM,
        scratch_shapes=[pltpu.VMEM((D, 256), BF)],
        compiler_params=params,
        cost_estimate=pl.CostEstimate(flops=2 * 128 * 256 * 4096, bytes_accessed=4 << 20, transcendentals=0),
    )(scal, xn, first, *others, sibling, state_pay)

    back4, back8 = by_chips(pay, 4), by_chips(pay, 8)
    near = jnp.concatenate([pay, back4], axis=0)
    far = jnp.concatenate([back4, back8], axis=0)
    own0 = jnp.concatenate([pay, back4, back8], axis=0)
    own1 = jnp.concatenate([by_chips(near, 1), by_chips(near, 2), by_chips(far, -1)], axis=0)
    sib0, sib1 = swap(own0), swap(own1)

    produced = pl.pallas_call(
        finish,
        name="finish",
        out_shape=shape(ROWS, COLS),
        in_specs=[SMEM, VMEM, VMEM, ANY] + [VMEM] * 7,
        out_specs=VMEM,
        scratch_shapes=[
            pltpu.VMEM((4, D, 256), BF),
            pltpu.VMEM((18 * ROWS, HD), BF),
            pltpu.VMEM((18 * ROWS, HD), BF),
            pltpu.VMEM((ROWS, 18 * ROWS), F32),
            pltpu.SemaphoreType.DMA((4,)),
        ],
        compiler_params=params,
        cost_estimate=pl.CostEstimate(flops=2 * 128 * 1024 * 8192, bytes_accessed=12 << 20, transcendentals=0),
    )(scal, hidden_in[0], xn, wq, own0, own1, sib0, sib1, yloc, aux, idc)
    moved = lax.ppermute(produced, "pipe", [(i, i + 1) for i in range(3)])
    return (produced[None], moved[None])


def solution(mesh):
    in_specs = (
        P("pipe", "ctx", "tp"),
        P("ctx"),
        P("pipe"),
        P("pipe", "tp"),
        P("pipe", "ctx", "tp"),
        P("pipe", "ctx", "tp"),
        P("pipe", "ctx", "tp"),
        P("pipe", "tp", None),
        P("pipe", "tp", None),
        P("pipe", "tp"),
        P("pipe", "tp"),
        P("pipe", "tp"),
    )
    out_specs = (P("pipe", "ctx", "tp"), P("pipe", "ctx", "tp"))
    return jax.shard_map(shards, mesh=mesh, in_specs=in_specs, out_specs=out_specs, check_vma=False)
```

```python
import jax
import jax.numpy as jnp
from jax import lax
from jax.experimental import pallas as pl
from jax.experimental.pallas import tpu as pltpu
from jax.sharding import PartitionSpec as P

D = 4096
HD = 128
ROWS = 128
COLS = 1024
CHIPS = 16
STATE = 16
HL = 16
WROWS = ROWS + 16
BACK = 8
NEG = -1e30
BF, F32 = jnp.bfloat16, jnp.float32
EXACT = lax.Precision.HIGHEST

W_FIRST = (-4, 0, 4, -8)
W_REL = tuple(a + b for b in (0, -1, 1) for a in W_FIRST) + (-6, -2, 2, 6)
KV_AT = {0: (0, 0), 4: (0, 1), 8: (0, 2), 1: (1, 0), 5: (1, 1), 2: (1, 2), 6: (1, 3), 3: (1, 4), 7: (1, 5)}


def iota(shape, dim):
    return lax.broadcasted_iota(jnp.int32, shape, dim)


def dot(a, b, precision=None):
    return jnp.dot(a, b, preferred_element_type=F32, precision=precision)


def pair(low, j, values):
    return jnp.where(low, values[:, 2 * j : 2 * j + 1], values[:, 2 * j + 1 : 2 * j + 2])


def front(scal, got, idc_ref, idr_ref, bias, rate, skip, xn, states, yloc, aux):
    attention, place = scal[0], scal[1]
    squares = jnp.zeros((ROWS, 1), F32)
    for s in range(4):
        hf = got[s, :ROWS, :].astype(F32)
        squares += jnp.sum(hf * hf, axis=1, keepdims=True)
    inverse = lax.rsqrt(squares / D + 1e-05)
    for s in range(4):
        gain = got[s, ROWS + 48 :, :].astype(F32)
        gain = gain[0:1] + gain[1:2] + gain[2:3]
        xn[:, s * COLS : (s + 1) * COLS] = (got[s, :ROWS, :].astype(F32) * inverse * gain).astype(BF)
    idc, idr = idc_ref[...], idr_ref[...]

    @pl.when(attention == 0)
    def _():
        maps = jnp.zeros((ROWS, 48), F32)
        for s in range(4):
            maps += lax.dot_general(
                xn[:, s * COLS : (s + 1) * COLS],
                got[s, ROWS : ROWS + 48, :],
                (((1,), (1,)), ((), ())),
                preferred_element_type=F32,
            )
        raw = maps[:, :HL] + bias[...]
        step = jnp.maximum(raw, 0.0) + jnp.log1p(jnp.exp(-jnp.abs(raw)))
        in_map, out_map = maps[:, HL : HL + STATE], maps[:, HL + STATE :]
        earlier = iota((ROWS, ROWS), 0) >= iota((ROWS, ROWS), 1)
        cum = dot(earlier.astype(F32), -step * rate[...], EXACT)
        empty = jnp.zeros((ROWS, ROWS - 32), F32)
        turned = jnp.concatenate([cum, in_map, empty], axis=1).T
        cum_t, in_t = turned[:HL], turned[HL : HL + STATE]
        both = dot(out_map, in_t, EXACT)
        mask = earlier & (idc == idr)
        last = cum[ROWS - 1 :, :]
        end = jnp.where(idc == idr[:, ROWS - 1 :], jnp.exp(last - cum), 0.0)
        low = iota((ROWS, ROWS), 1) < 64
        base = pl.multiple_of(place * COLS, COLS)
        for j in range(HL // 2):
            x = xn[:, pl.ds(base + j * 128, 128)].astype(F32)
            wx = x * pair(low, j, step)
            weights = [
                jnp.exp(jnp.where(mask, cum[:, i : i + 1] - cum_t[i : i + 1, :], NEG)) * both
                for i in (2 * j, 2 * j + 1)
            ]
            split = jnp.concatenate([jnp.where(low, wx, 0.0), jnp.where(low, 0.0, wx)], axis=0)
            inner = dot(jnp.concatenate(weights, axis=1), split, EXACT)
            yloc[:, j * 128 : (j + 1) * 128] = inner + pair(low[:1], j, skip[...]) * x
            state = dot(in_t, wx * pair(low, j, end), EXACT)
            at = 16 * (j // 2)
            states[at : at + 16, 128 * (j % 2) : 128 * (j % 2) + 128] = state.astype(BF)
        wide = jnp.concatenate([last, jnp.zeros((1, 256 - HL), F32)], axis=1)
        first = wide.astype(BF).astype(F32)
        second = (wide - first).astype(BF).astype(F32)
        third = wide - first - second
        row = iota((64, 256), 0)
        extra = jnp.where(row == 0, first, jnp.where(row == 1, second, jnp.where(row == 2, third, 0.0)))
        states[64:, :] = extra.astype(BF)
        aux[...] = jnp.concatenate([cum, out_map, empty], axis=1)


def project(scal, xn, own, sib, states, pay, kid, weight):
    attention, chip, core = scal[0], scal[2], scal[3]
    n = 0
    for r in range(BACK + 1):
        at = [w % CHIPS for w in W_REL].index(-r % CHIPS) * WROWS + ROWS
        for ref in (own, sib):
            kid[n : n + 1, :] = ref[at : at + 16, :ROWS].astype(F32)[0:1, :]
            n += 1

    @pl.when(attention == 1)
    def _():
        for n, rel in enumerate(W_REL):
            at = lax.rem(chip + rel + CHIPS, CHIPS) * 256
            rows = slice(n * WROWS, n * WROWS + ROWS)
            weight[pl.ds(pl.multiple_of(at + core * 128, 128), 128), :] = own[rows, :]
            weight[pl.ds(pl.multiple_of(at + (1 - core) * 128, 128), 128), :] = sib[rows, :]
        pay[...] = dot(xn[...], weight[...]).astype(BF)

    @pl.when(attention == 0)
    def _():
        pay[...] = states[...]


def query(scal, xn, wq, out, wbuf, sem):
    @pl.when(scal[0] == 1)
    def _():
        copies = [
            pltpu.make_async_copy(wq.at[:, pl.ds(j * 256, 256)], wbuf.at[j], sem.at[j]) for j in range(4)
        ]
        for copy in copies:
            copy.start()
        for j, copy in enumerate(copies):
            copy.wait()
            out[:, j * 256 : (j + 1) * 256] = dot(xn[...], wbuf[j]).astype(BF)


def attend(scal, h, q, blocks, kid, idc_ref, out, keys, values, mask):
    chip, core = scal[2], scal[3]
    idc = idc_ref[...]
    n = 0
    for r in range(BACK + 1):
        which, k = KV_AT[r]
        for mine in (True, False):
            ref = blocks[which if mine else 2 + which]
            rows = slice(n * ROWS, (n + 1) * ROWS)
            keys[rows, :] = ref[k * ROWS : (k + 1) * ROWS, :HD]
            values[rows, :] = ref[k * ROWS : (k + 1) * ROWS, HD:]
            allowed = idc == kid[n : n + 1, :]
            if r == 0 and mine:
                allowed = allowed & (iota((ROWS, ROWS), 0) >= iota((ROWS, ROWS), 1))
            else:
                valid = core == 1 if r == 0 else chip >= r
                allowed = allowed & (jnp.full((ROWS, ROWS), valid.astype(jnp.int32)) == 1)
            mask[:, rows] = jnp.where(allowed, 0.0, NEG)
            n += 1
    factor = HD ** (-0.5) * 1.4426950408889634
    for j in range(4):
        at = 256 * j
        rows = jnp.concatenate([q[:, at : at + HD], q[:, at + HD : at + 256]], axis=0)
        scores = lax.dot_general(
            rows, keys[...], (((1,), (1,)), ((), ())), preferred_element_type=F32
        )
        parts, dens = [], []
        for i in range(2):
            s = scores[i * ROWS : (i + 1) * ROWS, :] + mask[...]
            p = jnp.exp2((s - jnp.max(s, axis=1, keepdims=True)) * factor)
            dens.append(jnp.sum(p, axis=1, keepdims=True))
            parts.append(p.astype(BF))
        mixed = dot(jnp.concatenate(parts, axis=0), values[...])
        for i in range(2):
            o = (mixed[i * ROWS : (i + 1) * ROWS, :] / dens[i]).astype(BF).astype(F32)
            cols = slice(j * 256 + i * HD, j * 256 + (i + 1) * HD)
            out[:, cols] = (h[:, cols].astype(F32) + o).astype(BF)


def finish_states(scal, h, blocks, kid, yloc, aux, idc_ref, out):
    core, device = scal[3], scal[4]
    order = []
    for r in range(1, BACK + 1):
        def block(mine, back):
            which, k = KV_AT[back]
            return blocks[which if mine else 2 + which], k * ROWS, 2 * back + (0 if mine else 1)

        order.append((block(False, r - 1), block(False, r)))
        order.append((block(True, r), None))

    def read(entry, lo, hi):
        (ref, at, _), other = entry
        tile = ref[at + lo : at + hi, :].astype(F32)
        if other is not None:
            ref, at, _ = other
            tile = jnp.where(core == 1, tile, ref[at + lo : at + hi, :].astype(F32))
        return tile

    idc = idc_ref[...]
    before = jnp.zeros((1, HL), F32)
    coefs = []
    previous = None
    for k, entry in enumerate(order, 1):
        n = entry[0][2]
        tail = kid[n : n + 1, ROWS - 1 :]
        if entry[1] is not None:
            n = entry[1][2]
            tail = jnp.where(core == 1, tail, kid[n : n + 1, ROWS - 1 :])
        tail = jnp.where(device >= k, tail, -1.0)
        if previous is None:
            previous = tail
        fits = (tail == previous) & (tail >= 0.0)
        coefs.append(jnp.where(fits, jnp.exp(before), 0.0))
        extra = read(entry, 64, 80)
        before += extra[0:1, :HL] + extra[1:2, :HL] + extra[2:3, :HL]
    spread = (iota((HL, COLS), 1) // 64 == iota((HL, COLS), 0)).astype(F32)
    coef = dot(jnp.concatenate(coefs, axis=0), spread, EXACT)
    cum, out_map = aux[:, :HL], aux[:, HL : HL + STATE]
    reach = jnp.where(idc == previous, jnp.exp(cum), 0.0)
    low = iota((ROWS, ROWS), 1) < 64
    for c in range(4):
        incoming = jnp.zeros((STATE, 256), F32)
        for k, entry in enumerate(order):
            incoming += coef[k : k + 1, c * 256 : (c + 1) * 256] * read(entry, 16 * c, 16 * c + 16)
        for i in range(2):
            j = 2 * c + i
            cols = slice(j * 128, (j + 1) * 128)
            carried = dot(out_map, incoming[:, i * 128 : (i + 1) * 128], EXACT) * pair(low, j, reach)
            y = yloc[:, cols] + carried
            y2 = y * y
            one = jnp.sum(jnp.where(low, y2, 0.0), axis=1, keepdims=True)
            two = jnp.sum(jnp.where(low, 0.0, y2), axis=1, keepdims=True)
            scale = lax.rsqrt(jnp.where(low, one, two) / 64 + 1e-05)
            out[:, cols] = (h[:, cols].astype(F32) + y * scale).astype(BF)


def finish(scal, h, q, own0, own1, sib0, sib1, kid, yloc, aux, idc, out, keys, values, mask):
    blocks = (own0, own1, sib0, sib1)

    @pl.when(scal[0] == 1)
    def _():
        attend(scal, h, q, blocks, kid, idc, out, keys, values, mask)

    @pl.when(scal[0] == 0)
    def _():
        finish_states(scal, h, blocks, kid, yloc, aux, idc, out)


VMEM = pl.BlockSpec(memory_space=pltpu.VMEM)
SMEM = pl.BlockSpec(memory_space=pltpu.SMEM)
ANY = pl.BlockSpec(memory_space=pl.ANY)


def kernel(body, us, mib, outs, ins, scratch=()):
    return pl.pallas_call(
        body,
        name=body.__name__,
        out_shape=outs,
        in_specs=ins,
        out_specs=jax.tree.map(lambda _: VMEM, outs),
        scratch_shapes=scratch,
        compiler_params=pltpu.CompilerParams(vmem_limit_bytes=mib << 20),
        cost_estimate=pl.CostEstimate(flops=int(us * 1.15e9), bytes_accessed=1 << 20, transcendentals=0),
    )


def shape(*dims, dtype=BF):
    return jax.ShapeDtypeStruct(dims, dtype)


def by_chips(x, k):
    return lax.ppermute(x, "ctx", [(i, (i + 2 * k) % (2 * CHIPS)) for i in range(2 * CHIPS)])


def swap(x):
    return lax.ppermute(x, "ctx", [(i, i ^ 1) for i in range(2 * CHIPS)])


def shards(
    hidden_in,
    doc_ids,
    layer_kind,
    norm_gain,
    q_weight,
    k_weight,
    v_weight,
    bc_weight,
    dt_weight,
    dt_bias,
    decay_rate,
    skip_gain,
):
    device = lax.axis_index("ctx")
    scal = jnp.stack(
        [layer_kind[0], lax.axis_index("tp"), device // 2, device % 2, device]
    ).astype(jnp.int32)
    ids = doc_ids.astype(F32)
    idc, idr = ids[:, None], ids[None, :]

    wq = lax.all_gather(q_weight[0], "ctx", axis=0, tiled=True)

    gain = norm_gain[0]
    gain1 = lax.reduce_precision(gain, 8, 7)
    gain2 = lax.reduce_precision(gain - gain1, 8, 7)
    gain3 = gain - gain1 - gain2
    gains = jnp.concatenate([jnp.stack([gain1, gain2, gain3]), jnp.zeros((13, COLS), F32)]).astype(BF)
    everyone = lambda x: jnp.broadcast_to(x[None], (4,) + x.shape)
    parts = jnp.concatenate(
        [
            everyone(hidden_in[0]),
            dt_weight[0].T.reshape(4, HL, COLS),
            everyone(bc_weight[0].T),
            everyone(gains),
        ],
        axis=1,
    )
    wkv = jnp.concatenate([k_weight[0], v_weight[0]], axis=1)
    wkv = jnp.concatenate([wkv, jnp.pad(idr.astype(BF), ((0, 15), (0, 128)))], axis=0)
    a, b, c = [by_chips(wkv, k) for k in (4, -4, 8)]
    first = jnp.concatenate([a, wkv, b, c], axis=0)
    parts, first = lax.optimization_barrier((parts, first))
    got = lax.all_to_all(parts, "tp", 0, 0)
    xn, states, yloc, aux = kernel(
        front,
        4,
        20,
        (shape(ROWS, D), shape(ROWS, 256), shape(ROWS, COLS, dtype=F32), shape(ROWS, 128, dtype=F32)),
        [SMEM] + [VMEM] * 6,
    )(scal, got, idc, idr, dt_bias, decay_rate, skip_gain)

    others = [
        by_chips(first, 1),
        by_chips(first, -1),
        by_chips(first[: 2 * WROWS], 2),
        by_chips(first[WROWS : 3 * WROWS], -2),
    ]
    first, xn = lax.optimization_barrier((first, xn))
    weights = jnp.concatenate([first] + others, axis=0)
    sibling = swap(weights)

    pay, kid = kernel(
        project,
        2,
        12,
        (shape(ROWS, 256), shape(24, ROWS, dtype=F32)),
        [SMEM] + [VMEM] * 4,
        [pltpu.VMEM((D, 256), BF)],
    )(scal, xn, weights, sibling, states)
    q = kernel(
        query,
        5,
        52,
        shape(ROWS, COLS),
        [SMEM, VMEM, ANY],
        [pltpu.VMEM((4, D, 256), BF), pltpu.SemaphoreType.DMA((4,))],
    )(scal, xn, wq)

    back4, back8 = by_chips(pay, 4), by_chips(pay, 8)
    near = jnp.concatenate([pay, back4], axis=0)
    far = jnp.concatenate([back4, back8], axis=0)
    own0 = jnp.concatenate([pay, back4, back8], axis=0)
    own1 = jnp.concatenate([by_chips(near, 1), by_chips(near, 2), by_chips(far, -1)], axis=0)
    sib0, sib1 = swap(own0), swap(own1)

    produced = kernel(
        finish,
        6,
        32,
        shape(ROWS, COLS),
        [SMEM] + [VMEM] * 10,
        [
            pltpu.VMEM((18 * ROWS, HD), BF),
            pltpu.VMEM((18 * ROWS, HD), BF),
            pltpu.VMEM((ROWS, 18 * ROWS), F32),
        ],
    )(scal, hidden_in[0], q, own0, own1, sib0, sib1, kid, yloc, aux, idc)
    moved = lax.ppermute(produced, "pipe", [(i, i + 1) for i in range(3)])
    return (produced[None], moved[None])


def solution(mesh):
    in_specs = (
        P("pipe", "ctx", "tp"),
        P("ctx"),
        P("pipe"),
        P("pipe", "tp"),
        P("pipe", "ctx", "tp"),
        P("pipe", "ctx", "tp"),
        P("pipe", "ctx", "tp"),
        P("pipe", "tp", None),
        P("pipe", "tp", None),
        P("pipe", "tp"),
        P("pipe", "tp"),
        P("pipe", "tp"),
    )
    out_specs = (P("pipe", "ctx", "tp"), P("pipe", "ctx", "tp"))
    return jax.shard_map(shards, mesh=mesh, in_specs=in_specs, out_specs=out_specs, check_vma=False)
```

```python
import jax
import jax.numpy as jnp
from jax import lax
from jax.experimental import pallas as pl
from jax.experimental.pallas import tpu as pltpu
from jax.sharding import PartitionSpec as P

D = 4096
HD = 128
ROWS = 128
COLS = 1024
CHIPS = 16
STATE = 16
HL = 16
WROWS = ROWS + 16
BACK = 8
NEG = -1e30
BF, F32 = jnp.bfloat16, jnp.float32
EXACT = lax.Precision.HIGHEST

W_FIRST = (-4, 0, 4, -8)
W_REL = tuple(a + b for b in (0, -1, 1, 2) for a in W_FIRST)
KV_AT = (0, 3, 5, 7, 1, 4, 6, 8, 2)


def iota(shape, dim):
    return lax.broadcasted_iota(jnp.int32, shape, dim)


def dot(a, b, precision=None):
    return jnp.dot(a, b, preferred_element_type=F32, precision=precision)


def pair(low, j, values):
    return jnp.where(low, values[:, 2 * j : 2 * j + 1], values[:, 2 * j + 1 : 2 * j + 2])


def front(scal, got, idc_ref, idr_ref, bias, rate, skip, xn, states, yloc, aux):
    attention, place = scal[0], scal[1]
    squares = jnp.zeros((ROWS, 1), F32)
    for s in range(4):
        hf = got[s, :ROWS, :].astype(F32)
        squares += jnp.sum(hf * hf, axis=1, keepdims=True)
    inverse = lax.rsqrt(squares / D + 1e-05)
    for s in range(4):
        gain = got[s, ROWS + 48 :, :].astype(F32)
        gain = gain[0:1] + gain[1:2] + gain[2:3]
        xn[:, s * COLS : (s + 1) * COLS] = (got[s, :ROWS, :].astype(F32) * inverse * gain).astype(BF)
    idc, idr = idc_ref[...], idr_ref[...]

    @pl.when(attention == 0)
    def _():
        maps = jnp.zeros((ROWS, 48), F32)
        for s in range(4):
            maps += lax.dot_general(
                xn[:, s * COLS : (s + 1) * COLS],
                got[s, ROWS : ROWS + 48, :],
                (((1,), (1,)), ((), ())),
                preferred_element_type=F32,
            )
        raw = maps[:, :HL] + bias[...]
        step = jnp.maximum(raw, 0.0) + jnp.log1p(jnp.exp(-jnp.abs(raw)))
        in_map, out_map = maps[:, HL : HL + STATE], maps[:, HL + STATE :]
        earlier = iota((ROWS, ROWS), 0) >= iota((ROWS, ROWS), 1)
        cum = dot(earlier.astype(F32), -step * rate[...], EXACT)
        empty = jnp.zeros((ROWS, ROWS - 32), F32)
        turned = jnp.concatenate([cum, in_map, empty], axis=1).T
        cum_t, in_t = turned[:HL], turned[HL : HL + STATE]
        both = dot(out_map, in_t, EXACT)
        mask = earlier & (idc == idr)
        last = cum[ROWS - 1 :, :]
        end = jnp.where(idc == idr[:, ROWS - 1 :], jnp.exp(last - cum), 0.0)
        low = iota((ROWS, ROWS), 1) < 64
        base = pl.multiple_of(place * COLS, COLS)
        for j in range(HL // 2):
            x = xn[:, pl.ds(base + j * 128, 128)].astype(F32)
            wx = x * pair(low, j, step)
            weights = [
                jnp.exp(jnp.where(mask, cum[:, i : i + 1] - cum_t[i : i + 1, :], NEG)) * both
                for i in (2 * j, 2 * j + 1)
            ]
            split = jnp.concatenate([jnp.where(low, wx, 0.0), jnp.where(low, 0.0, wx)], axis=0)
            inner = dot(jnp.concatenate(weights, axis=1), split, EXACT)
            yloc[:, j * 128 : (j + 1) * 128] = inner + pair(low[:1], j, skip[...]) * x
            state = dot(in_t, wx * pair(low, j, end), EXACT)
            at = 16 * (j // 2)
            states[at : at + 16, 128 * (j % 2) : 128 * (j % 2) + 128] = state.astype(BF)
        wide = jnp.concatenate([last, jnp.zeros((1, 256 - HL), F32)], axis=1)
        first = wide.astype(BF).astype(F32)
        second = (wide - first).astype(BF).astype(F32)
        third = wide - first - second
        row = iota((64, 256), 0)
        extra = jnp.where(row == 0, first, jnp.where(row == 1, second, jnp.where(row == 2, third, 0.0)))
        states[64:, :] = extra.astype(BF)
        aux[...] = jnp.concatenate([cum, out_map, empty], axis=1)


def project(scal, xn, own, sib, states, pay, kid, weight):
    attention, chip, core = scal[0], scal[2], scal[3]
    n = 0
    for r in range(BACK + 1):
        at = [w % CHIPS for w in W_REL].index(-r % CHIPS) * WROWS + ROWS
        for ref in (own, sib):
            kid[n : n + 1, :] = ref[at : at + 16, :ROWS].astype(F32)[0:1, :]
            n += 1

    @pl.when(attention == 1)
    def _():
        for n, rel in enumerate(W_REL):
            at = lax.rem(chip + rel + CHIPS, CHIPS) * 256
            rows = slice(n * WROWS, n * WROWS + ROWS)
            weight[pl.ds(pl.multiple_of(at + core * 128, 128), 128), :] = own[rows, :]
            weight[pl.ds(pl.multiple_of(at + (1 - core) * 128, 128), 128), :] = sib[rows, :]
        pay[...] = dot(xn[...], weight[...]).astype(BF)

    @pl.when(attention == 0)
    def _():
        pay[...] = states[...]


def query(scal, xn, wq, out, wbuf, sem):
    @pl.when(scal[0] == 1)
    def _():
        copies = [
            pltpu.make_async_copy(wq.at[:, pl.ds(j * 256, 256)], wbuf.at[j], sem.at[j]) for j in range(4)
        ]
        for copy in copies:
            copy.start()
        for j, copy in enumerate(copies):
            copy.wait()
            out[:, j * 256 : (j + 1) * 256] = dot(xn[...], wbuf[j]).astype(BF)


def attend(pairs, h, q, keys, values, mask, out):
    factor = HD ** (-0.5) * 1.4426950408889634
    for j in pairs:
        at = 256 * j
        rows = jnp.concatenate([q[:, at : at + HD], q[:, at + HD : at + 256]], axis=0)
        scores = lax.dot_general(
            rows, keys[...], (((1,), (1,)), ((), ())), preferred_element_type=F32
        )
        parts, dens = [], []
        for i in range(2):
            s = scores[i * ROWS : (i + 1) * ROWS, :] + mask[...]
            p = jnp.exp2((s - jnp.max(s, axis=1, keepdims=True)) * factor)
            dens.append(jnp.sum(p, axis=1, keepdims=True))
            parts.append(p.astype(BF))
        mixed = dot(jnp.concatenate(parts, axis=0), values[...])
        for i in range(2):
            o = (mixed[i * ROWS : (i + 1) * ROWS, :] / dens[i]).astype(BF).astype(F32)
            cols = slice(at + i * HD, at + (i + 1) * HD)
            out[:, at - 256 * pairs[0] + i * HD : at - 256 * pairs[0] + (i + 1) * HD] = (h[:, cols].astype(F32) + o).astype(BF)


def assemble(scal, own, sib, kid, aux, idc_ref, keys, values, mask, incoming, reach):
    idc = idc_ref[...]
    chip, core, device = scal[2], scal[3], scal[4]

    @pl.when(scal[0] == 1)
    def _():
        n = 0
        for r in range(BACK + 1):
            k = KV_AT[r]
            for mine in (True, False):
                ref = own if mine else sib
                rows = slice(n * ROWS, (n + 1) * ROWS)
                keys[rows, :] = ref[k * ROWS : (k + 1) * ROWS, :HD]
                values[rows, :] = ref[k * ROWS : (k + 1) * ROWS, HD:]
                allowed = idc == kid[n : n + 1, :]
                if r == 0 and mine:
                    allowed = allowed & (iota((ROWS, ROWS), 0) >= iota((ROWS, ROWS), 1))
                else:
                    valid = core == 1 if r == 0 else chip >= r
                    allowed = allowed & (jnp.full((ROWS, ROWS), valid.astype(jnp.int32)) == 1)
                mask[:, rows] = jnp.where(allowed, 0.0, NEG)
                n += 1

    @pl.when(scal[0] == 0)
    def _():
        def block(mine, back):
            return own if mine else sib, KV_AT[back] * ROWS, 2 * back + (0 if mine else 1)

        order = []
        for r in range(1, BACK + 1):
            order.append((block(False, r - 1), block(False, r)))
            order.append((block(True, r), None))

        def read(entry, lo, hi):
            (ref, at, _), other = entry
            tile = ref[at + lo : at + hi, :].astype(F32)
            if other is not None:
                ref, at, _ = other
                tile = jnp.where(core == 1, tile, ref[at + lo : at + hi, :].astype(F32))
            return tile

        before = jnp.zeros((1, HL), F32)
        coefs = []
        previous = None
        for k, entry in enumerate(order, 1):
            tails = [kid[e[2] : e[2] + 1, ROWS - 1 :] for e in entry if e is not None]
            tail = tails[0] if len(tails) == 1 else jnp.where(core == 1, tails[0], tails[1])
            tail = jnp.where(device >= k, tail, -1.0)
            if previous is None:
                previous = tail
            fits = (tail == previous) & (tail >= 0.0)
            coefs.append(jnp.where(fits, jnp.exp(before), 0.0))
            extra = read(entry, 64, 80)
            before += extra[0:1, :HL] + extra[1:2, :HL] + extra[2:3, :HL]
        spread = (iota((HL, COLS), 1) // 64 == iota((HL, COLS), 0)).astype(F32)
        coef = dot(jnp.concatenate(coefs, axis=0), spread, EXACT)
        for c in range(4):
            total = jnp.zeros((STATE, 256), F32)
            for k, entry in enumerate(order):
                total += coef[k : k + 1, c * 256 : (c + 1) * 256] * read(entry, 16 * c, 16 * c + 16)
            incoming[:, c * 256 : (c + 1) * 256] = total
        cum = aux[:, :HL]
        wide = jnp.where(idc == previous, jnp.exp(cum), 0.0)
        reach[...] = jnp.concatenate([wide, jnp.zeros((ROWS, ROWS - HL), F32)], axis=1)


def finish_states(pairs, h, yloc, aux, incoming, reach_ref, out):
    out_map, reach = aux[:, HL : HL + STATE], reach_ref[:, :HL]
    low = iota((ROWS, ROWS), 1) < 64
    for n in range(2 * len(pairs)):
        j = 2 * pairs[0] + n
        cols = slice(j * 128, (j + 1) * 128)
        carried = dot(out_map, incoming[:, cols], EXACT) * pair(low, j, reach)
        y = yloc[:, cols] + carried
        y2 = y * y
        one = jnp.sum(jnp.where(low, y2, 0.0), axis=1, keepdims=True)
        two = jnp.sum(jnp.where(low, 0.0, y2), axis=1, keepdims=True)
        scale = lax.rsqrt(jnp.where(low, one, two) / 64 + 1e-05)
        out[:, n * 128 : (n + 1) * 128] = (h[:, cols].astype(F32) + y * scale).astype(BF)


def finish(pairs, scal, h, q, keys, values, mask, yloc, aux, incoming, reach, out):
    @pl.when(scal[0] == 1)
    def _():
        attend(pairs, h, q, keys, values, mask, out)

    @pl.when(scal[0] == 0)
    def _():
        finish_states(pairs, h, yloc, aux, incoming, reach, out)


def finish_low(*refs):
    finish((0, 1, 2), *refs)


def finish_high(*refs):
    finish((3,), *refs)


VMEM = pl.BlockSpec(memory_space=pltpu.VMEM)
SMEM = pl.BlockSpec(memory_space=pltpu.SMEM)
ANY = pl.BlockSpec(memory_space=pl.ANY)


def kernel(body, us, mib, outs, ins, scratch=()):
    return pl.pallas_call(
        body,
        name=body.__name__,
        out_shape=outs,
        in_specs=ins,
        out_specs=jax.tree.map(lambda _: VMEM, outs),
        scratch_shapes=scratch,
        compiler_params=pltpu.CompilerParams(vmem_limit_bytes=mib << 20),
        cost_estimate=pl.CostEstimate(flops=int(us * 1.15e9), bytes_accessed=1 << 20, transcendentals=0),
    )


def shape(*dims, dtype=BF):
    return jax.ShapeDtypeStruct(dims, dtype)


def by_chips(x, k):
    return lax.ppermute(x, "ctx", [(i, (i + 2 * k) % (2 * CHIPS)) for i in range(2 * CHIPS)])


def swap(x):
    return lax.ppermute(x, "ctx", [(i, i ^ 1) for i in range(2 * CHIPS)])


def shards(
    hidden_in,
    doc_ids,
    layer_kind,
    norm_gain,
    q_weight,
    k_weight,
    v_weight,
    bc_weight,
    dt_weight,
    dt_bias,
    decay_rate,
    skip_gain,
):
    device = lax.axis_index("ctx")
    scal = jnp.stack(
        [layer_kind[0], lax.axis_index("tp"), device // 2, device % 2, device]
    ).astype(jnp.int32)
    ids = doc_ids.astype(F32)
    idc, idr = ids[:, None], ids[None, :]

    wq = lax.all_gather(q_weight[0], "ctx", axis=0, tiled=True)

    gain = norm_gain[0]
    gain1 = lax.reduce_precision(gain, 8, 7)
    gain2 = lax.reduce_precision(gain - gain1, 8, 7)
    gain3 = gain - gain1 - gain2
    gains = jnp.concatenate([jnp.stack([gain1, gain2, gain3]), jnp.zeros((13, COLS), F32)]).astype(BF)
    everyone = lambda x: jnp.broadcast_to(x[None], (4,) + x.shape)
    parts = jnp.concatenate(
        [
            everyone(hidden_in[0]),
            dt_weight[0].T.reshape(4, HL, COLS),
            everyone(bc_weight[0].T),
            everyone(gains),
        ],
        axis=1,
    )
    wkv = jnp.concatenate([k_weight[0], v_weight[0]], axis=1)
    wkv = jnp.concatenate([wkv, jnp.pad(idr.astype(BF), ((0, 15), (0, 128)))], axis=0)
    a, b, c = [by_chips(wkv, k) for k in (4, -4, 8)]
    first = jnp.concatenate([a, wkv, b, c], axis=0)
    parts, first = lax.optimization_barrier((parts, first))
    got = lax.all_to_all(parts, "tp", 0, 0)
    xn, states, yloc, aux = kernel(
        front,
        4,
        20,
        (shape(ROWS, D), shape(ROWS, 256), shape(ROWS, COLS, dtype=F32), shape(ROWS, 128, dtype=F32)),
        [SMEM] + [VMEM] * 6,
    )(scal, got, idc, idr, dt_bias, decay_rate, skip_gain)

    others = [by_chips(first, k) for k in (1, -1, -2)]
    first, xn = lax.optimization_barrier((first, xn))
    weights = jnp.concatenate([first] + others, axis=0)
    sibling = swap(weights)

    pay, kid = kernel(
        project,
        2,
        12,
        (shape(ROWS, 256), shape(24, ROWS, dtype=F32)),
        [SMEM] + [VMEM] * 4,
        [pltpu.VMEM((D, 256), BF)],
    )(scal, xn, weights, sibling, states)
    q = kernel(
        query,
        5,
        52,
        shape(ROWS, COLS),
        [SMEM, VMEM, ANY],
        [pltpu.VMEM((4, D, 256), BF), pltpu.SemaphoreType.DMA((4,))],
    )(scal, xn, wq)

    back4, back8 = by_chips(pay, 4), by_chips(pay, 8)
    near = jnp.concatenate([pay, back4], axis=0)
    far = jnp.concatenate([back4, back8], axis=0)
    own = jnp.concatenate(
        [pay, back4, back8, by_chips(near, 1), by_chips(near, 2), by_chips(far, -1)], axis=0
    )
    sib = swap(own)
    sib, q = lax.optimization_barrier((sib, q))

    gathered = kernel(
        assemble,
        1,
        16,
        (
            shape(18 * ROWS, HD),
            shape(18 * ROWS, HD),
            shape(ROWS, 18 * ROWS, dtype=F32),
            shape(STATE, COLS, dtype=F32),
            shape(ROWS, ROWS, dtype=F32),
        ),
        [SMEM] + [VMEM] * 5,
    )(scal, own, sib, kid, aux, idc)
    keys, values, mask, incoming, reach = gathered
    made, moved = [], []
    for body, us, cols in ((finish_low, 4, 768), (finish_high, 2, 256)):
        part = kernel(body, us, 20, shape(ROWS, cols), [SMEM] + [VMEM] * 9)(
            scal, hidden_in[0], q, keys, values, mask, yloc, aux, incoming, reach
        )
        made.append(part)
        q, part = lax.optimization_barrier((q, part))
        moved.append(lax.ppermute(part, "pipe", [(i, i + 1) for i in range(3)]))
    produced, moved = jnp.concatenate(made, axis=1), jnp.concatenate(moved, axis=1)
    return (produced[None], moved[None])


def solution(mesh):
    in_specs = (
        P("pipe", "ctx", "tp"),
        P("ctx"),
        P("pipe"),
        P("pipe", "tp"),
        P("pipe", "ctx", "tp"),
        P("pipe", "ctx", "tp"),
        P("pipe", "ctx", "tp"),
        P("pipe", "tp", None),
        P("pipe", "tp", None),
        P("pipe", "tp"),
        P("pipe", "tp"),
        P("pipe", "tp"),
    )
    out_specs = (P("pipe", "ctx", "tp"), P("pipe", "ctx", "tp"))
    return jax.shard_map(shards, mesh=mesh, in_specs=in_specs, out_specs=out_specs, check_vma=False)
```

```python
import jax
import jax.numpy as jnp
from jax import lax
from jax.experimental import pallas as pl
from jax.experimental.pallas import tpu as pltpu
from jax.sharding import PartitionSpec as P

D = 4096
HD = 128
ROWS = 128
COLS = 1024
CHIPS = 16
STATE = 16
HL = 16
WROWS = ROWS + 16
BACK = 8
NEG = -1e30
BF, F32 = jnp.bfloat16, jnp.float32
EXACT = lax.Precision.HIGHEST

W_FIRST = (-4, 0, 4, -8)
W_REL = tuple(a + b for b in (0, -1, 1) for a in W_FIRST) + (-6, -2, 2, 6)
KV_AT = (0, 3, 5, 7, 1, 4, 6, 8, 2)


def iota(shape, dim):
    return lax.broadcasted_iota(jnp.int32, shape, dim)


def dot(a, b, precision=None):
    return jnp.dot(a, b, preferred_element_type=F32, precision=precision)


def pair(low, j, values):
    return jnp.where(low, values[:, 2 * j : 2 * j + 1], values[:, 2 * j + 1 : 2 * j + 2])


def front(scal, got, idc_ref, idr_ref, bias, rate, skip, xn, states, yloc, aux):
    attention, place = scal[0], scal[1]
    squares = jnp.zeros((ROWS, 1), F32)
    for s in range(4):
        hf = got[s, :ROWS, :].astype(F32)
        squares += jnp.sum(hf * hf, axis=1, keepdims=True)
    inverse = lax.rsqrt(squares / D + 1e-05)
    for s in range(4):
        gain = got[s, ROWS + 48 :, :].astype(F32)
        gain = gain[0:1] + gain[1:2] + gain[2:3]
        xn[:, s * COLS : (s + 1) * COLS] = (got[s, :ROWS, :].astype(F32) * inverse * gain).astype(BF)
    idc, idr = idc_ref[...], idr_ref[...]

    @pl.when(attention == 0)
    def _():
        maps = jnp.zeros((ROWS, 48), F32)
        for s in range(4):
            maps += lax.dot_general(
                xn[:, s * COLS : (s + 1) * COLS],
                got[s, ROWS : ROWS + 48, :],
                (((1,), (1,)), ((), ())),
                preferred_element_type=F32,
            )
        raw = maps[:, :HL] + bias[...]
        step = jnp.maximum(raw, 0.0) + jnp.log1p(jnp.exp(-jnp.abs(raw)))
        in_map, out_map = maps[:, HL : HL + STATE], maps[:, HL + STATE :]
        earlier = iota((ROWS, ROWS), 0) >= iota((ROWS, ROWS), 1)
        cum = dot(earlier.astype(F32), -step * rate[...], EXACT)
        empty = jnp.zeros((ROWS, ROWS - 32), F32)
        turned = jnp.concatenate([cum, in_map, empty], axis=1).T
        cum_t, in_t = turned[:HL], turned[HL : HL + STATE]
        both = dot(out_map, in_t, EXACT)
        mask = earlier & (idc == idr)
        last = cum[ROWS - 1 :, :]
        end = jnp.where(idc == idr[:, ROWS - 1 :], jnp.exp(last - cum), 0.0)
        low = iota((ROWS, ROWS), 1) < 64
        base = pl.multiple_of(place * COLS, COLS)
        for j in range(HL // 2):
            x = xn[:, pl.ds(base + j * 128, 128)].astype(F32)
            wx = x * pair(low, j, step)
            weights = [
                jnp.exp(jnp.where(mask, cum[:, i : i + 1] - cum_t[i : i + 1, :], NEG)) * both
                for i in (2 * j, 2 * j + 1)
            ]
            split = jnp.concatenate([jnp.where(low, wx, 0.0), jnp.where(low, 0.0, wx)], axis=0)
            inner = dot(jnp.concatenate(weights, axis=1), split, EXACT)
            yloc[:, j * 128 : (j + 1) * 128] = inner + pair(low[:1], j, skip[...]) * x
            state = dot(in_t, wx * pair(low, j, end), EXACT)
            at = 16 * (j // 2)
            states[at : at + 16, 128 * (j % 2) : 128 * (j % 2) + 128] = state.astype(BF)
        wide = jnp.concatenate([last, jnp.zeros((1, 256 - HL), F32)], axis=1)
        first = wide.astype(BF).astype(F32)
        second = (wide - first).astype(BF).astype(F32)
        third = wide - first - second
        row = iota((64, 256), 0)
        extra = jnp.where(row == 0, first, jnp.where(row == 1, second, jnp.where(row == 2, third, 0.0)))
        states[64:, :] = extra.astype(BF)
        aux[...] = jnp.concatenate([cum, out_map, empty], axis=1)


def project(scal, xn, own, sib, states, pay, kid, weight):
    attention, chip, core = scal[0], scal[2], scal[3]
    n = 0
    for r in range(BACK + 1):
        at = [w % CHIPS for w in W_REL].index(-r % CHIPS) * WROWS + ROWS
        for ref in (own, sib):
            kid[n : n + 1, :] = ref[at : at + 16, :ROWS].astype(F32)[0:1, :]
            n += 1

    @pl.when(attention == 1)
    def _():
        for n, rel in enumerate(W_REL):
            at = lax.rem(chip + rel + CHIPS, CHIPS) * 256
            rows = slice(n * WROWS, n * WROWS + ROWS)
            weight[pl.ds(pl.multiple_of(at + core * 128, 128), 128), :] = own[rows, :]
            weight[pl.ds(pl.multiple_of(at + (1 - core) * 128, 128), 128), :] = sib[rows, :]
        pay[...] = dot(xn[...], weight[...]).astype(BF)

    @pl.when(attention == 0)
    def _():
        pay[...] = states[...]


def query(scal, xn, wq, out, wbuf, sem):
    @pl.when(scal[0] == 1)
    def _():
        copies = [
            pltpu.make_async_copy(wq.at[:, pl.ds(j * 256, 256)], wbuf.at[j], sem.at[j]) for j in range(4)
        ]
        for copy in copies:
            copy.start()
        for j, copy in enumerate(copies):
            copy.wait()
            out[:, j * 256 : (j + 1) * 256] = dot(xn[...], wbuf[j]).astype(BF)


def attend(pairs, h, q, keys, values, mask, out):
    factor = HD ** (-0.5) * 1.4426950408889634
    for j in pairs:
        at = 256 * j
        rows = jnp.concatenate([q[:, at : at + HD], q[:, at + HD : at + 256]], axis=0)
        scores = lax.dot_general(
            rows, keys[...], (((1,), (1,)), ((), ())), preferred_element_type=F32
        )
        parts, dens = [], []
        for i in range(2):
            s = scores[i * ROWS : (i + 1) * ROWS, :] + mask[...]
            p = jnp.exp2((s - jnp.max(s, axis=1, keepdims=True)) * factor)
            dens.append(jnp.sum(p, axis=1, keepdims=True))
            parts.append(p.astype(BF))
        mixed = dot(jnp.concatenate(parts, axis=0), values[...])
        for i in range(2):
            o = (mixed[i * ROWS : (i + 1) * ROWS, :] / dens[i]).astype(BF).astype(F32)
            cols = slice(at + i * HD, at + (i + 1) * HD)
            out[:, at - 256 * pairs[0] + i * HD : at - 256 * pairs[0] + (i + 1) * HD] = (h[:, cols].astype(F32) + o).astype(BF)


def assemble(scal, own, sib, kid, aux, idc_ref, keys, values, mask, incoming, reach):
    idc = idc_ref[...]
    chip, core, device = scal[2], scal[3], scal[4]

    @pl.when(scal[0] == 1)
    def _():
        n = 0
        for r in range(BACK + 1):
            k = KV_AT[r]
            for mine in (True, False):
                ref = own if mine else sib
                rows = slice(n * ROWS, (n + 1) * ROWS)
                keys[rows, :] = ref[k * ROWS : (k + 1) * ROWS, :HD]
                values[rows, :] = ref[k * ROWS : (k + 1) * ROWS, HD:]
                allowed = idc == kid[n : n + 1, :]
                if r == 0 and mine:
                    allowed = allowed & (iota((ROWS, ROWS), 0) >= iota((ROWS, ROWS), 1))
                else:
                    valid = core == 1 if r == 0 else chip >= r
                    allowed = allowed & (jnp.full((ROWS, ROWS), valid.astype(jnp.int32)) == 1)
                mask[:, rows] = jnp.where(allowed, 0.0, NEG)
                n += 1

    @pl.when(scal[0] == 0)
    def _():
        def block(mine, back):
            return own if mine else sib, KV_AT[back] * ROWS, 2 * back + (0 if mine else 1)

        order = []
        for r in range(1, BACK + 1):
            order.append((block(False, r - 1), block(False, r)))
            order.append((block(True, r), None))

        def read(entry, lo, hi):
            (ref, at, _), other = entry
            tile = ref[at + lo : at + hi, :].astype(F32)
            if other is not None:
                ref, at, _ = other
                tile = jnp.where(core == 1, tile, ref[at + lo : at + hi, :].astype(F32))
            return tile

        before = jnp.zeros((1, HL), F32)
        coefs = []
        previous = None
        for k, entry in enumerate(order, 1):
            tails = [kid[e[2] : e[2] + 1, ROWS - 1 :] for e in entry if e is not None]
            tail = tails[0] if len(tails) == 1 else jnp.where(core == 1, tails[0], tails[1])
            tail = jnp.where(device >= k, tail, -1.0)
            if previous is None:
                previous = tail
            fits = (tail == previous) & (tail >= 0.0)
            coefs.append(jnp.where(fits, jnp.exp(before), 0.0))
            extra = read(entry, 64, 80)
            before += extra[0:1, :HL] + extra[1:2, :HL] + extra[2:3, :HL]
        spread = (iota((HL, COLS), 1) // 64 == iota((HL, COLS), 0)).astype(F32)
        coef = dot(jnp.concatenate(coefs, axis=0), spread, EXACT)
        for c in range(4):
            total = jnp.zeros((STATE, 256), F32)
            for k, entry in enumerate(order):
                total += coef[k : k + 1, c * 256 : (c + 1) * 256] * read(entry, 16 * c, 16 * c + 16)
            incoming[:, c * 256 : (c + 1) * 256] = total
        cum = aux[:, :HL]
        wide = jnp.where(idc == previous, jnp.exp(cum), 0.0)
        reach[...] = jnp.concatenate([wide, jnp.zeros((ROWS, ROWS - HL), F32)], axis=1)


def finish_states(pairs, h, yloc, aux, incoming, reach_ref, out):
    out_map, reach = aux[:, HL : HL + STATE], reach_ref[:, :HL]
    low = iota((ROWS, ROWS), 1) < 64
    for n in range(2 * len(pairs)):
        j = 2 * pairs[0] + n
        cols = slice(j * 128, (j + 1) * 128)
        carried = dot(out_map, incoming[:, cols], EXACT) * pair(low, j, reach)
        y = yloc[:, cols] + carried
        y2 = y * y
        one = jnp.sum(jnp.where(low, y2, 0.0), axis=1, keepdims=True)
        two = jnp.sum(jnp.where(low, 0.0, y2), axis=1, keepdims=True)
        scale = lax.rsqrt(jnp.where(low, one, two) / 64 + 1e-05)
        out[:, n * 128 : (n + 1) * 128] = (h[:, cols].astype(F32) + y * scale).astype(BF)


def finish(pairs, scal, h, q, keys, values, mask, yloc, aux, incoming, reach, out):
    @pl.when(scal[0] == 1)
    def _():
        attend(pairs, h, q, keys, values, mask, out)

    @pl.when(scal[0] == 0)
    def _():
        finish_states(pairs, h, yloc, aux, incoming, reach, out)


def finish_low(*refs):
    finish((0, 1, 2), *refs)


def finish_high(*refs):
    finish((3,), *refs)


VMEM = pl.BlockSpec(memory_space=pltpu.VMEM)
SMEM = pl.BlockSpec(memory_space=pltpu.SMEM)
ANY = pl.BlockSpec(memory_space=pl.ANY)


def kernel(body, us, mib, outs, ins, scratch=()):
    return pl.pallas_call(
        body,
        name=body.__name__,
        out_shape=outs,
        in_specs=ins,
        out_specs=jax.tree.map(lambda _: VMEM, outs),
        scratch_shapes=scratch,
        compiler_params=pltpu.CompilerParams(vmem_limit_bytes=mib << 20),
        cost_estimate=pl.CostEstimate(flops=int(us * 1.15e9), bytes_accessed=1 << 20, transcendentals=0),
    )


def shape(*dims, dtype=BF):
    return jax.ShapeDtypeStruct(dims, dtype)


def by_chips(x, k):
    return lax.ppermute(x, "ctx", [(i, (i + 2 * k) % (2 * CHIPS)) for i in range(2 * CHIPS)])


def swap(x):
    return lax.ppermute(x, "ctx", [(i, i ^ 1) for i in range(2 * CHIPS)])


def shards(
    hidden_in,
    doc_ids,
    layer_kind,
    norm_gain,
    q_weight,
    k_weight,
    v_weight,
    bc_weight,
    dt_weight,
    dt_bias,
    decay_rate,
    skip_gain,
):
    device = lax.axis_index("ctx")
    scal = jnp.stack(
        [layer_kind[0], lax.axis_index("tp"), device // 2, device % 2, device]
    ).astype(jnp.int32)
    ids = doc_ids.astype(F32)
    idc, idr = ids[:, None], ids[None, :]

    wq = lax.all_gather(q_weight[0], "ctx", axis=0, tiled=True)

    gain = norm_gain[0]
    gain1 = lax.reduce_precision(gain, 8, 7)
    gain2 = lax.reduce_precision(gain - gain1, 8, 7)
    gain3 = gain - gain1 - gain2
    gains = jnp.concatenate([jnp.stack([gain1, gain2, gain3]), jnp.zeros((13, COLS), F32)]).astype(BF)
    everyone = lambda x: jnp.broadcast_to(x[None], (4,) + x.shape)
    parts = jnp.concatenate(
        [
            everyone(hidden_in[0]),
            dt_weight[0].T.reshape(4, HL, COLS),
            everyone(bc_weight[0].T),
            everyone(gains),
        ],
        axis=1,
    )
    wkv = jnp.concatenate([k_weight[0], v_weight[0]], axis=1)
    wkv = jnp.concatenate([wkv, jnp.pad(idr.astype(BF), ((0, 15), (0, 128)))], axis=0)
    a, b, c = [by_chips(wkv, k) for k in (4, -4, 8)]
    first = jnp.concatenate([a, wkv, b, c], axis=0)
    parts, first = lax.optimization_barrier((parts, first))
    got = lax.all_to_all(parts, "tp", 0, 0)
    xn, states, yloc, aux = kernel(
        front,
        4,
        20,
        (shape(ROWS, D), shape(ROWS, 256), shape(ROWS, COLS, dtype=F32), shape(ROWS, 128, dtype=F32)),
        [SMEM] + [VMEM] * 6,
    )(scal, got, idc, idr, dt_bias, decay_rate, skip_gain)

    others = [
        by_chips(first, 1),
        by_chips(first, -1),
        by_chips(first[: 2 * WROWS], 2),
        by_chips(first[WROWS : 3 * WROWS], -2),
    ]
    first, xn = lax.optimization_barrier((first, xn))
    weights = jnp.concatenate([first] + others, axis=0)
    sibling = swap(weights)

    pay, kid = kernel(
        project,
        2,
        12,
        (shape(ROWS, 256), shape(24, ROWS, dtype=F32)),
        [SMEM] + [VMEM] * 4,
        [pltpu.VMEM((D, 256), BF)],
    )(scal, xn, weights, sibling, states)
    q = kernel(
        query,
        5,
        52,
        shape(ROWS, COLS),
        [SMEM, VMEM, ANY],
        [pltpu.VMEM((4, D, 256), BF), pltpu.SemaphoreType.DMA((4,))],
    )(scal, xn, wq)

    back4, back8 = by_chips(pay, 4), by_chips(pay, 8)
    near = jnp.concatenate([pay, back4], axis=0)
    far = jnp.concatenate([back4, back8], axis=0)
    own = jnp.concatenate(
        [pay, back4, back8, by_chips(near, 1), by_chips(near, 2), by_chips(far, -1)], axis=0
    )
    sib = swap(own)
    sib, q = lax.optimization_barrier((sib, q))

    gathered = kernel(
        assemble,
        1,
        16,
        (
            shape(18 * ROWS, HD),
            shape(18 * ROWS, HD),
            shape(ROWS, 18 * ROWS, dtype=F32),
            shape(STATE, COLS, dtype=F32),
            shape(ROWS, ROWS, dtype=F32),
        ),
        [SMEM] + [VMEM] * 5,
    )(scal, own, sib, kid, aux, idc)
    keys, values, mask, incoming, reach = gathered
    made, moved = [], []
    for body, us, cols in ((finish_low, 4, 768), (finish_high, 2, 256)):
        part = kernel(body, us, 20, shape(ROWS, cols), [SMEM] + [VMEM] * 9)(
            scal, hidden_in[0], q, keys, values, mask, yloc, aux, incoming, reach
        )
        made.append(part)
        q, part = lax.optimization_barrier((q, part))
        moved.append(lax.ppermute(part, "pipe", [(i, i + 1) for i in range(3)]))
    produced, moved = jnp.concatenate(made, axis=1), jnp.concatenate(moved, axis=1)
    return (produced[None], moved[None])


def solution(mesh):
    in_specs = (
        P("pipe", "ctx", "tp"),
        P("ctx"),
        P("pipe"),
        P("pipe", "tp"),
        P("pipe", "ctx", "tp"),
        P("pipe", "ctx", "tp"),
        P("pipe", "ctx", "tp"),
        P("pipe", "tp", None),
        P("pipe", "tp", None),
        P("pipe", "tp"),
        P("pipe", "tp"),
        P("pipe", "tp"),
    )
    out_specs = (P("pipe", "ctx", "tp"), P("pipe", "ctx", "tp"))
    return jax.shard_map(shards, mesh=mesh, in_specs=in_specs, out_specs=out_specs, check_vma=False)
```

```python
import jax
import jax.numpy as jnp
from jax import lax
from jax.experimental import pallas as pl
from jax.experimental.pallas import tpu as pltpu
from jax.sharding import PartitionSpec as P

D = 4096
HD = 128
ROWS = 128
COLS = 1024
CHIPS = 16
STATE = 16
HL = 16
WROWS = ROWS + 16
BACK = 8
NEG = -1e30
BF, F32 = jnp.bfloat16, jnp.float32
EXACT = lax.Precision.HIGHEST

W_FIRST = (-4, 0, 4, -8)
W_REL = W_FIRST + (-6, -2, 2, 6) + tuple(a + b for b in (-1, 1) for a in W_FIRST)
KV_AT = (0, 5, 3, 7, 1, 6, 4, 8, 2)


def iota(shape, dim):
    return lax.broadcasted_iota(jnp.int32, shape, dim)


def dot(a, b, precision=None):
    return jnp.dot(a, b, preferred_element_type=F32, precision=precision)


def pair(low, j, values):
    return jnp.where(low, values[:, 2 * j : 2 * j + 1], values[:, 2 * j + 1 : 2 * j + 2])


def front(scal, got, idc_ref, idr_ref, bias, rate, skip, xn, states, yloc, aux):
    attention, place = scal[0], scal[1]
    squares = jnp.zeros((ROWS, 1), F32)
    for s in range(4):
        hf = got[s, :ROWS, :].astype(F32)
        squares += jnp.sum(hf * hf, axis=1, keepdims=True)
    inverse = lax.rsqrt(squares / D + 1e-05)
    for s in range(4):
        gain = got[s, ROWS + 48 :, :].astype(F32)
        gain = gain[0:1] + gain[1:2] + gain[2:3]
        xn[:, s * COLS : (s + 1) * COLS] = (got[s, :ROWS, :].astype(F32) * inverse * gain).astype(BF)
    idc, idr = idc_ref[...], idr_ref[...]

    @pl.when(attention == 0)
    def _():
        maps = jnp.zeros((ROWS, 48), F32)
        for s in range(4):
            maps += lax.dot_general(
                xn[:, s * COLS : (s + 1) * COLS],
                got[s, ROWS : ROWS + 48, :],
                (((1,), (1,)), ((), ())),
                preferred_element_type=F32,
            )
        raw = maps[:, :HL] + bias[...]
        step = jnp.maximum(raw, 0.0) + jnp.log1p(jnp.exp(-jnp.abs(raw)))
        in_map, out_map = maps[:, HL : HL + STATE], maps[:, HL + STATE :]
        earlier = iota((ROWS, ROWS), 0) >= iota((ROWS, ROWS), 1)
        cum = dot(earlier.astype(F32), -step * rate[...], EXACT)
        empty = jnp.zeros((ROWS, ROWS - 32), F32)
        turned = jnp.concatenate([cum, in_map, empty], axis=1).T
        cum_t, in_t = turned[:HL], turned[HL : HL + STATE]
        both = dot(out_map, in_t, EXACT)
        mask = earlier & (idc == idr)
        last = cum[ROWS - 1 :, :]
        end = jnp.where(idc == idr[:, ROWS - 1 :], jnp.exp(last - cum), 0.0)
        low = iota((ROWS, ROWS), 1) < 64
        base = pl.multiple_of(place * COLS, COLS)
        for j in range(HL // 2):
            x = xn[:, pl.ds(base + j * 128, 128)].astype(F32)
            wx = x * pair(low, j, step)
            weights = [
                jnp.exp(jnp.where(mask, cum[:, i : i + 1] - cum_t[i : i + 1, :], NEG)) * both
                for i in (2 * j, 2 * j + 1)
            ]
            split = jnp.concatenate([jnp.where(low, wx, 0.0), jnp.where(low, 0.0, wx)], axis=0)
            inner = dot(jnp.concatenate(weights, axis=1), split, EXACT)
            yloc[:, j * 128 : (j + 1) * 128] = inner + pair(low[:1], j, skip[...]) * x
            state = dot(in_t, wx * pair(low, j, end), EXACT)
            at = 16 * (j // 2)
            states[at : at + 16, 128 * (j % 2) : 128 * (j % 2) + 128] = state.astype(BF)
        wide = jnp.concatenate([last, jnp.zeros((1, 256 - HL), F32)], axis=1)
        first = wide.astype(BF).astype(F32)
        second = (wide - first).astype(BF).astype(F32)
        third = wide - first - second
        row = iota((64, 256), 0)
        extra = jnp.where(row == 0, first, jnp.where(row == 1, second, jnp.where(row == 2, third, 0.0)))
        states[64:, :] = extra.astype(BF)
        aux[...] = jnp.concatenate([cum, out_map, empty], axis=1)


def project(scal, xn, own, sib, states, pay, kid, weight):
    attention, chip, core = scal[0], scal[2], scal[3]
    n = 0
    for r in range(BACK + 1):
        at = [w % CHIPS for w in W_REL].index(-r % CHIPS) * WROWS + ROWS
        for ref in (own, sib):
            kid[n : n + 1, :] = ref[at : at + 16, :ROWS].astype(F32)[0:1, :]
            n += 1

    @pl.when(attention == 1)
    def _():
        for n, rel in enumerate(W_REL):
            at = lax.rem(chip + rel + CHIPS, CHIPS) * 256
            rows = slice(n * WROWS, n * WROWS + ROWS)
            weight[pl.ds(pl.multiple_of(at + core * 128, 128), 128), :] = own[rows, :]
            weight[pl.ds(pl.multiple_of(at + (1 - core) * 128, 128), 128), :] = sib[rows, :]
        pay[...] = dot(xn[...], weight[...]).astype(BF)

    @pl.when(attention == 0)
    def _():
        pay[...] = states[...]


def query(scal, xn, wq, out, wbuf, sem):
    @pl.when(scal[0] == 1)
    def _():
        copies = [
            pltpu.make_async_copy(wq.at[:, pl.ds(j * 256, 256)], wbuf.at[j], sem.at[j]) for j in range(4)
        ]
        for copy in copies:
            copy.start()
        for j, copy in enumerate(copies):
            copy.wait()
            out[:, j * 256 : (j + 1) * 256] = dot(xn[...], wbuf[j]).astype(BF)


def attend(pairs, h, q, keys, values, mask, out):
    factor = HD ** (-0.5) * 1.4426950408889634
    for j in pairs:
        at = 256 * j
        rows = jnp.concatenate([q[:, at : at + HD], q[:, at + HD : at + 256]], axis=0)
        scores = lax.dot_general(
            rows, keys[...], (((1,), (1,)), ((), ())), preferred_element_type=F32
        )
        parts, dens = [], []
        for i in range(2):
            s = scores[i * ROWS : (i + 1) * ROWS, :] + mask[...]
            p = jnp.exp2((s - jnp.max(s, axis=1, keepdims=True)) * factor)
            dens.append(jnp.sum(p, axis=1, keepdims=True))
            parts.append(p.astype(BF))
        mixed = dot(jnp.concatenate(parts, axis=0), values[...])
        for i in range(2):
            o = (mixed[i * ROWS : (i + 1) * ROWS, :] / dens[i]).astype(BF).astype(F32)
            cols = slice(at + i * HD, at + (i + 1) * HD)
            out[:, at - 256 * pairs[0] + i * HD : at - 256 * pairs[0] + (i + 1) * HD] = (h[:, cols].astype(F32) + o).astype(BF)


def assemble(scal, own, sib, kid, aux, idc_ref, keys, values, mask, incoming, reach):
    idc = idc_ref[...]
    chip, core, device = scal[2], scal[3], scal[4]

    @pl.when(scal[0] == 1)
    def _():
        n = 0
        for r in range(BACK + 1):
            k = KV_AT[r]
            for mine in (True, False):
                ref = own if mine else sib
                rows = slice(n * ROWS, (n + 1) * ROWS)
                keys[rows, :] = ref[k * ROWS : (k + 1) * ROWS, :HD]
                values[rows, :] = ref[k * ROWS : (k + 1) * ROWS, HD:]
                allowed = idc == kid[n : n + 1, :]
                if r == 0 and mine:
                    allowed = allowed & (iota((ROWS, ROWS), 0) >= iota((ROWS, ROWS), 1))
                else:
                    valid = core == 1 if r == 0 else chip >= r
                    allowed = allowed & (jnp.full((ROWS, ROWS), valid.astype(jnp.int32)) == 1)
                mask[:, rows] = jnp.where(allowed, 0.0, NEG)
                n += 1

    @pl.when(scal[0] == 0)
    def _():
        def block(mine, back):
            return own if mine else sib, KV_AT[back] * ROWS, 2 * back + (0 if mine else 1)

        order = []
        for r in range(1, BACK + 1):
            order.append((block(False, r - 1), block(False, r)))
            order.append((block(True, r), None))

        def read(entry, lo, hi):
            (ref, at, _), other = entry
            tile = ref[at + lo : at + hi, :].astype(F32)
            if other is not None:
                ref, at, _ = other
                tile = jnp.where(core == 1, tile, ref[at + lo : at + hi, :].astype(F32))
            return tile

        before = jnp.zeros((1, HL), F32)
        coefs = []
        previous = None
        for k, entry in enumerate(order, 1):
            tails = [kid[e[2] : e[2] + 1, ROWS - 1 :] for e in entry if e is not None]
            tail = tails[0] if len(tails) == 1 else jnp.where(core == 1, tails[0], tails[1])
            tail = jnp.where(device >= k, tail, -1.0)
            if previous is None:
                previous = tail
            fits = (tail == previous) & (tail >= 0.0)
            coefs.append(jnp.where(fits, jnp.exp(before), 0.0))
            extra = read(entry, 64, 80)
            before += extra[0:1, :HL] + extra[1:2, :HL] + extra[2:3, :HL]
        spread = (iota((HL, COLS), 1) // 64 == iota((HL, COLS), 0)).astype(F32)
        coef = dot(jnp.concatenate(coefs, axis=0), spread, EXACT)
        for c in range(4):
            total = jnp.zeros((STATE, 256), F32)
            for k, entry in enumerate(order):
                total += coef[k : k + 1, c * 256 : (c + 1) * 256] * read(entry, 16 * c, 16 * c + 16)
            incoming[:, c * 256 : (c + 1) * 256] = total
        cum = aux[:, :HL]
        wide = jnp.where(idc == previous, jnp.exp(cum), 0.0)
        reach[...] = jnp.concatenate([wide, jnp.zeros((ROWS, ROWS - HL), F32)], axis=1)


def finish_states(pairs, h, yloc, aux, incoming, reach_ref, out):
    out_map, reach = aux[:, HL : HL + STATE], reach_ref[:, :HL]
    low = iota((ROWS, ROWS), 1) < 64
    for n in range(2 * len(pairs)):
        j = 2 * pairs[0] + n
        cols = slice(j * 128, (j + 1) * 128)
        carried = dot(out_map, incoming[:, cols], EXACT) * pair(low, j, reach)
        y = yloc[:, cols] + carried
        y2 = y * y
        one = jnp.sum(jnp.where(low, y2, 0.0), axis=1, keepdims=True)
        two = jnp.sum(jnp.where(low, 0.0, y2), axis=1, keepdims=True)
        scale = lax.rsqrt(jnp.where(low, one, two) / 64 + 1e-05)
        out[:, n * 128 : (n + 1) * 128] = (h[:, cols].astype(F32) + y * scale).astype(BF)


def finish(pairs, scal, h, q, keys, values, mask, yloc, aux, incoming, reach, out):
    @pl.when(scal[0] == 1)
    def _():
        attend(pairs, h, q, keys, values, mask, out)

    @pl.when(scal[0] == 0)
    def _():
        finish_states(pairs, h, yloc, aux, incoming, reach, out)


def finish_low(*refs):
    finish((0, 1, 2), *refs)


def finish_high(*refs):
    finish((3,), *refs)


VMEM = pl.BlockSpec(memory_space=pltpu.VMEM)
SMEM = pl.BlockSpec(memory_space=pltpu.SMEM)
ANY = pl.BlockSpec(memory_space=pl.ANY)


def kernel(body, us, mib, outs, ins, scratch=()):
    return pl.pallas_call(
        body,
        name=body.__name__,
        out_shape=outs,
        in_specs=ins,
        out_specs=jax.tree.map(lambda _: VMEM, outs),
        scratch_shapes=scratch,
        compiler_params=pltpu.CompilerParams(vmem_limit_bytes=mib << 20),
        cost_estimate=pl.CostEstimate(flops=int(us * 1.15e9), bytes_accessed=1 << 20, transcendentals=0),
    )


def shape(*dims, dtype=BF):
    return jax.ShapeDtypeStruct(dims, dtype)


def by_chips(x, k):
    return lax.ppermute(x, "ctx", [(i, (i + 2 * k) % (2 * CHIPS)) for i in range(2 * CHIPS)])


def swap(x):
    return lax.ppermute(x, "ctx", [(i, i ^ 1) for i in range(2 * CHIPS)])


def shards(
    hidden_in,
    doc_ids,
    layer_kind,
    norm_gain,
    q_weight,
    k_weight,
    v_weight,
    bc_weight,
    dt_weight,
    dt_bias,
    decay_rate,
    skip_gain,
):
    device = lax.axis_index("ctx")
    scal = jnp.stack(
        [layer_kind[0], lax.axis_index("tp"), device // 2, device % 2, device]
    ).astype(jnp.int32)
    ids = doc_ids.astype(F32)
    idc, idr = ids[:, None], ids[None, :]

    wq = lax.all_gather(q_weight[0], "ctx", axis=0, tiled=True)

    gain = norm_gain[0]
    gain1 = lax.reduce_precision(gain, 8, 7)
    gain2 = lax.reduce_precision(gain - gain1, 8, 7)
    gain3 = gain - gain1 - gain2
    gains = jnp.concatenate([jnp.stack([gain1, gain2, gain3]), jnp.zeros((13, COLS), F32)]).astype(BF)
    everyone = lambda x: jnp.broadcast_to(x[None], (4,) + x.shape)
    parts = jnp.concatenate(
        [
            everyone(hidden_in[0]),
            dt_weight[0].T.reshape(4, HL, COLS),
            everyone(bc_weight[0].T),
            everyone(gains),
        ],
        axis=1,
    )
    wkv = jnp.concatenate([k_weight[0], v_weight[0]], axis=1)
    wkv = jnp.concatenate([wkv, jnp.pad(idr.astype(BF), ((0, 15), (0, 128)))], axis=0)
    a, b, c = [by_chips(wkv, k) for k in (4, -4, 8)]
    first = jnp.concatenate([a, wkv, b, c], axis=0)
    halves = [jnp.concatenate([a, wkv], axis=0), jnp.concatenate([wkv, b], axis=0)]
    parts, first, halves = lax.optimization_barrier((parts, first, halves))
    got = lax.all_to_all(parts, "tp", 0, 0)
    xn, states, yloc, aux = kernel(
        front,
        4,
        20,
        (shape(ROWS, D), shape(ROWS, 256), shape(ROWS, COLS, dtype=F32), shape(ROWS, 128, dtype=F32)),
        [SMEM] + [VMEM] * 6,
    )(scal, got, idc, idr, dt_bias, decay_rate, skip_gain)

    others = [
        by_chips(halves[0], 2),
        by_chips(halves[1], -2),
        by_chips(first, 1),
        by_chips(first, -1),
    ]
    first, xn = lax.optimization_barrier((first, xn))
    weights = jnp.concatenate([first] + others, axis=0)
    sibling = swap(weights)

    pay, kid = kernel(
        project,
        2,
        12,
        (shape(ROWS, 256), shape(24, ROWS, dtype=F32)),
        [SMEM] + [VMEM] * 4,
        [pltpu.VMEM((D, 256), BF)],
    )(scal, xn, weights, sibling, states)

    back4, back8 = by_chips(pay, 4), by_chips(pay, 8)
    near = jnp.concatenate([pay, back4], axis=0)
    far = jnp.concatenate([back4, back8], axis=0)
    near2 = by_chips(near, 2)
    xn, near2 = lax.optimization_barrier((xn, near2))
    q = kernel(
        query,
        5,
        52,
        shape(ROWS, COLS),
        [SMEM, VMEM, ANY],
        [pltpu.VMEM((4, D, 256), BF), pltpu.SemaphoreType.DMA((4,))],
    )(scal, xn, wq)
    pay, q = lax.optimization_barrier((pay, q))
    own = jnp.concatenate(
        [pay, back4, back8, near2, by_chips(near, 1), by_chips(far, -1)], axis=0
    )
    sib = swap(own)

    gathered = kernel(
        assemble,
        1,
        16,
        (
            shape(18 * ROWS, HD),
            shape(18 * ROWS, HD),
            shape(ROWS, 18 * ROWS, dtype=F32),
            shape(STATE, COLS, dtype=F32),
            shape(ROWS, ROWS, dtype=F32),
        ),
        [SMEM] + [VMEM] * 5,
    )(scal, own, sib, kid, aux, idc)
    keys, values, mask, incoming, reach = gathered
    made, moved = [], []
    for body, us, cols in ((finish_low, 4, 768), (finish_high, 2, 256)):
        part = kernel(body, us, 20, shape(ROWS, cols), [SMEM] + [VMEM] * 9)(
            scal, hidden_in[0], q, keys, values, mask, yloc, aux, incoming, reach
        )
        made.append(part)
        q, part = lax.optimization_barrier((q, part))
        moved.append(lax.ppermute(part, "pipe", [(i, i + 1) for i in range(3)]))
    produced, moved = jnp.concatenate(made, axis=1), jnp.concatenate(moved, axis=1)
    return (produced[None], moved[None])


def solution(mesh):
    in_specs = (
        P("pipe", "ctx", "tp"),
        P("ctx"),
        P("pipe"),
        P("pipe", "tp"),
        P("pipe", "ctx", "tp"),
        P("pipe", "ctx", "tp"),
        P("pipe", "ctx", "tp"),
        P("pipe", "tp", None),
        P("pipe", "tp", None),
        P("pipe", "tp"),
        P("pipe", "tp"),
        P("pipe", "tp"),
    )
    out_specs = (P("pipe", "ctx", "tp"), P("pipe", "ctx", "tp"))
    return jax.shard_map(shards, mesh=mesh, in_specs=in_specs, out_specs=out_specs, check_vma=False)
```

```python
import jax
import jax.numpy as jnp
from jax import lax
from jax.experimental import pallas as pl
from jax.experimental.pallas import tpu as pltpu
from jax.sharding import PartitionSpec as P

D = 4096
HD = 128
ROWS = 128
COLS = 1024
CHIPS = 16
STATE = 16
HL = 16
WROWS = ROWS + 16
BACK = 8
NEG = -1e30
BF, F32 = jnp.bfloat16, jnp.float32
EXACT = lax.Precision.HIGHEST

W_FIRST = (-4, 0, 4, -8)
W_REL = tuple(a + b for b in (0, -1, 1) for a in W_FIRST) + (-6, -2, 2, 6)
KV_AT = (0, 5, 3, 7, 1, 6, 4, 8, 2)


def iota(shape, dim):
    return lax.broadcasted_iota(jnp.int32, shape, dim)


def dot(a, b, precision=None):
    return jnp.dot(a, b, preferred_element_type=F32, precision=precision)


def pair(low, j, values):
    return jnp.where(low, values[:, 2 * j : 2 * j + 1], values[:, 2 * j + 1 : 2 * j + 2])


def front(scal, got, idc_ref, idr_ref, bias, rate, skip, xn, states, yloc, aux):
    attention, place = scal[0], scal[1]
    squares = jnp.zeros((ROWS, 1), F32)
    for s in range(4):
        hf = got[s, :ROWS, :].astype(F32)
        squares += jnp.sum(hf * hf, axis=1, keepdims=True)
    inverse = lax.rsqrt(squares / D + 1e-05)
    for s in range(4):
        gain = got[s, ROWS + 48 :, :].astype(F32)
        gain = gain[0:1] + gain[1:2] + gain[2:3]
        xn[:, s * COLS : (s + 1) * COLS] = (got[s, :ROWS, :].astype(F32) * inverse * gain).astype(BF)
    idc, idr = idc_ref[...], idr_ref[...]

    @pl.when(attention == 0)
    def _():
        maps = jnp.zeros((ROWS, 48), F32)
        for s in range(4):
            maps += lax.dot_general(
                xn[:, s * COLS : (s + 1) * COLS],
                got[s, ROWS : ROWS + 48, :],
                (((1,), (1,)), ((), ())),
                preferred_element_type=F32,
            )
        raw = maps[:, :HL] + bias[...]
        step = jnp.maximum(raw, 0.0) + jnp.log1p(jnp.exp(-jnp.abs(raw)))
        in_map, out_map = maps[:, HL : HL + STATE], maps[:, HL + STATE :]
        earlier = iota((ROWS, ROWS), 0) >= iota((ROWS, ROWS), 1)
        cum = dot(earlier.astype(F32), -step * rate[...], EXACT)
        empty = jnp.zeros((ROWS, ROWS - 32), F32)
        turned = jnp.concatenate([cum, in_map, empty], axis=1).T
        cum_t, in_t = turned[:HL], turned[HL : HL + STATE]
        both = dot(out_map, in_t, EXACT)
        mask = earlier & (idc == idr)
        last = cum[ROWS - 1 :, :]
        end = jnp.where(idc == idr[:, ROWS - 1 :], jnp.exp(last - cum), 0.0)
        low = iota((ROWS, ROWS), 1) < 64
        base = pl.multiple_of(place * COLS, COLS)
        for j in range(HL // 2):
            x = xn[:, pl.ds(base + j * 128, 128)].astype(F32)
            wx = x * pair(low, j, step)
            weights = [
                jnp.exp(jnp.where(mask, cum[:, i : i + 1] - cum_t[i : i + 1, :], NEG)) * both
                for i in (2 * j, 2 * j + 1)
            ]
            split = jnp.concatenate([jnp.where(low, wx, 0.0), jnp.where(low, 0.0, wx)], axis=0)
            inner = dot(jnp.concatenate(weights, axis=1), split, EXACT)
            yloc[:, j * 128 : (j + 1) * 128] = inner + pair(low[:1], j, skip[...]) * x
            state = dot(in_t, wx * pair(low, j, end), EXACT)
            at = 16 * (j // 2)
            states[at : at + 16, 128 * (j % 2) : 128 * (j % 2) + 128] = state.astype(BF)
        wide = jnp.concatenate([last, jnp.zeros((1, 256 - HL), F32)], axis=1)
        first = wide.astype(BF).astype(F32)
        second = (wide - first).astype(BF).astype(F32)
        third = wide - first - second
        row = iota((64, 256), 0)
        extra = jnp.where(row == 0, first, jnp.where(row == 1, second, jnp.where(row == 2, third, 0.0)))
        states[64:, :] = extra.astype(BF)
        aux[...] = jnp.concatenate([cum, out_map, empty], axis=1)


def project(scal, xn, own, sib, states, pay, kid, weight):
    attention, chip, core = scal[0], scal[2], scal[3]
    n = 0
    for r in range(BACK + 1):
        at = [w % CHIPS for w in W_REL].index(-r % CHIPS) * WROWS + ROWS
        for ref in (own, sib):
            kid[n : n + 1, :] = ref[at : at + 16, :ROWS].astype(F32)[0:1, :]
            n += 1

    @pl.when(attention == 1)
    def _():
        for n, rel in enumerate(W_REL):
            at = lax.rem(chip + rel + CHIPS, CHIPS) * 256
            rows = slice(n * WROWS, n * WROWS + ROWS)
            weight[pl.ds(pl.multiple_of(at + core * 128, 128), 128), :] = own[rows, :]
            weight[pl.ds(pl.multiple_of(at + (1 - core) * 128, 128), 128), :] = sib[rows, :]
        pay[...] = dot(xn[...], weight[...]).astype(BF)

    @pl.when(attention == 0)
    def _():
        pay[...] = states[...]


def query(scal, xn, wq, out, wbuf, total, sem):
    @pl.when(scal[0] == 1)
    def _():
        parts = [slice(j * 512, (j + 1) * 512) for j in range(8)]
        copies = [
            pltpu.make_async_copy(wq.at[part, :], wbuf.at[part, :], sem.at[j]) for j, part in enumerate(parts)
        ]
        for copy in copies:
            copy.start()
        for j, (copy, part) in enumerate(zip(copies, parts)):
            copy.wait()
            product = dot(xn[:, part], wbuf[part, :])
            total[...] = product if j == 0 else total[...] + product
        out[...] = total[...].astype(BF)


def attend(pairs, h, q, keys, values, mask, out):
    factor = HD ** (-0.5) * 1.4426950408889634
    for j in pairs:
        at = 256 * j
        rows = jnp.concatenate([q[:, at : at + HD], q[:, at + HD : at + 256]], axis=0)
        scores = lax.dot_general(
            rows, keys[...], (((1,), (1,)), ((), ())), preferred_element_type=F32
        )
        parts, dens = [], []
        for i in range(2):
            s = scores[i * ROWS : (i + 1) * ROWS, :] + mask[...]
            p = jnp.exp2((s - jnp.max(s, axis=1, keepdims=True)) * factor)
            dens.append(jnp.sum(p, axis=1, keepdims=True))
            parts.append(p.astype(BF))
        mixed = dot(jnp.concatenate(parts, axis=0), values[...])
        for i in range(2):
            o = (mixed[i * ROWS : (i + 1) * ROWS, :] / dens[i]).astype(BF).astype(F32)
            cols = slice(at + i * HD, at + (i + 1) * HD)
            out[:, at - 256 * pairs[0] + i * HD : at - 256 * pairs[0] + (i + 1) * HD] = (h[:, cols].astype(F32) + o).astype(BF)


def assemble(scal, own, sib, kid, aux, idc_ref, keys, values, mask, incoming, reach):
    idc = idc_ref[...]
    chip, core, device = scal[2], scal[3], scal[4]

    @pl.when(scal[0] == 1)
    def _():
        n = 0
        for r in range(BACK + 1):
            k = KV_AT[r]
            for mine in (True, False):
                ref = own if mine else sib
                rows = slice(n * ROWS, (n + 1) * ROWS)
                keys[rows, :] = ref[k * ROWS : (k + 1) * ROWS, :HD]
                values[rows, :] = ref[k * ROWS : (k + 1) * ROWS, HD:]
                allowed = idc == kid[n : n + 1, :]
                if r == 0 and mine:
                    allowed = allowed & (iota((ROWS, ROWS), 0) >= iota((ROWS, ROWS), 1))
                else:
                    valid = core == 1 if r == 0 else chip >= r
                    allowed = allowed & (jnp.full((ROWS, ROWS), valid.astype(jnp.int32)) == 1)
                mask[:, rows] = jnp.where(allowed, 0.0, NEG)
                n += 1

    @pl.when(scal[0] == 0)
    def _():
        def block(mine, back):
            return own if mine else sib, KV_AT[back] * ROWS, 2 * back + (0 if mine else 1)

        order = []
        for r in range(1, BACK + 1):
            order.append((block(False, r - 1), block(False, r)))
            order.append((block(True, r), None))

        def read(entry, lo, hi):
            (ref, at, _), other = entry
            tile = ref[at + lo : at + hi, :].astype(F32)
            if other is not None:
                ref, at, _ = other
                tile = jnp.where(core == 1, tile, ref[at + lo : at + hi, :].astype(F32))
            return tile

        before = jnp.zeros((1, HL), F32)
        coefs = []
        previous = None
        for k, entry in enumerate(order, 1):
            tails = [kid[e[2] : e[2] + 1, ROWS - 1 :] for e in entry if e is not None]
            tail = tails[0] if len(tails) == 1 else jnp.where(core == 1, tails[0], tails[1])
            tail = jnp.where(device >= k, tail, -1.0)
            if previous is None:
                previous = tail
            fits = (tail == previous) & (tail >= 0.0)
            coefs.append(jnp.where(fits, jnp.exp(before), 0.0))
            extra = read(entry, 64, 80)
            before += extra[0:1, :HL] + extra[1:2, :HL] + extra[2:3, :HL]
        spread = (iota((HL, COLS), 1) // 64 == iota((HL, COLS), 0)).astype(F32)
        coef = dot(jnp.concatenate(coefs, axis=0), spread, EXACT)
        for c in range(4):
            total = jnp.zeros((STATE, 256), F32)
            for k, entry in enumerate(order):
                total += coef[k : k + 1, c * 256 : (c + 1) * 256] * read(entry, 16 * c, 16 * c + 16)
            incoming[:, c * 256 : (c + 1) * 256] = total
        cum = aux[:, :HL]
        wide = jnp.where(idc == previous, jnp.exp(cum), 0.0)
        reach[...] = jnp.concatenate([wide, jnp.zeros((ROWS, ROWS - HL), F32)], axis=1)


def finish_states(pairs, h, yloc, aux, incoming, reach_ref, out):
    out_map, reach = aux[:, HL : HL + STATE], reach_ref[:, :HL]
    low = iota((ROWS, ROWS), 1) < 64
    for n in range(2 * len(pairs)):
        j = 2 * pairs[0] + n
        cols = slice(j * 128, (j + 1) * 128)
        carried = dot(out_map, incoming[:, cols], EXACT) * pair(low, j, reach)
        y = yloc[:, cols] + carried
        y2 = y * y
        one = jnp.sum(jnp.where(low, y2, 0.0), axis=1, keepdims=True)
        two = jnp.sum(jnp.where(low, 0.0, y2), axis=1, keepdims=True)
        scale = lax.rsqrt(jnp.where(low, one, two) / 64 + 1e-05)
        out[:, n * 128 : (n + 1) * 128] = (h[:, cols].astype(F32) + y * scale).astype(BF)


def finish(pairs, scal, h, q, keys, values, mask, yloc, aux, incoming, reach, out):
    @pl.when(scal[0] == 1)
    def _():
        attend(pairs, h, q, keys, values, mask, out)

    @pl.when(scal[0] == 0)
    def _():
        finish_states(pairs, h, yloc, aux, incoming, reach, out)


def finish_low(*refs):
    finish((0, 1, 2), *refs)


def finish_high(*refs):
    finish((3,), *refs)


VMEM = pl.BlockSpec(memory_space=pltpu.VMEM)
SMEM = pl.BlockSpec(memory_space=pltpu.SMEM)
ANY = pl.BlockSpec(memory_space=pl.ANY)


def kernel(body, us, mib, outs, ins, scratch=()):
    return pl.pallas_call(
        body,
        name=body.__name__,
        out_shape=outs,
        in_specs=ins,
        out_specs=jax.tree.map(lambda _: VMEM, outs),
        scratch_shapes=scratch,
        compiler_params=pltpu.CompilerParams(vmem_limit_bytes=mib << 20),
        cost_estimate=pl.CostEstimate(flops=int(us * 1.15e9), bytes_accessed=1 << 20, transcendentals=0),
    )


def shape(*dims, dtype=BF):
    return jax.ShapeDtypeStruct(dims, dtype)


def by_chips(x, k):
    return lax.ppermute(x, "ctx", [(i, (i + 2 * k) % (2 * CHIPS)) for i in range(2 * CHIPS)])


def swap(x):
    return lax.ppermute(x, "ctx", [(i, i ^ 1) for i in range(2 * CHIPS)])


def shards(
    hidden_in,
    doc_ids,
    layer_kind,
    norm_gain,
    q_weight,
    k_weight,
    v_weight,
    bc_weight,
    dt_weight,
    dt_bias,
    decay_rate,
    skip_gain,
):
    device = lax.axis_index("ctx")
    scal = jnp.stack(
        [layer_kind[0], lax.axis_index("tp"), device // 2, device % 2, device]
    ).astype(jnp.int32)
    ids = doc_ids.astype(F32)
    idc, idr = ids[:, None], ids[None, :]

    wq = lax.all_gather(q_weight[0], "ctx", axis=0, tiled=True)

    gain = norm_gain[0]
    gain1 = lax.reduce_precision(gain, 8, 7)
    gain2 = lax.reduce_precision(gain - gain1, 8, 7)
    gain3 = gain - gain1 - gain2
    gains = jnp.concatenate([jnp.stack([gain1, gain2, gain3]), jnp.zeros((13, COLS), F32)]).astype(BF)
    everyone = lambda x: jnp.broadcast_to(x[None], (4,) + x.shape)
    parts = jnp.concatenate(
        [
            everyone(hidden_in[0]),
            dt_weight[0].T.reshape(4, HL, COLS),
            everyone(bc_weight[0].T),
            everyone(gains),
        ],
        axis=1,
    )
    wkv = jnp.concatenate([k_weight[0], v_weight[0]], axis=1)
    wkv = jnp.concatenate([wkv, jnp.pad(idr.astype(BF), ((0, 15), (0, 128)))], axis=0)
    a, b, c = [by_chips(wkv, k) for k in (4, -4, 8)]
    first = jnp.concatenate([a, wkv, b, c], axis=0)
    halves = [jnp.concatenate([a, wkv], axis=0), jnp.concatenate([wkv, b], axis=0)]
    parts, first, halves = lax.optimization_barrier((parts, first, halves))
    got = lax.all_to_all(parts, "tp", 0, 0)
    xn, states, yloc, aux = kernel(
        front,
        4,
        20,
        (shape(ROWS, D), shape(ROWS, 256), shape(ROWS, COLS, dtype=F32), shape(ROWS, 128, dtype=F32)),
        [SMEM] + [VMEM] * 6,
    )(scal, got, idc, idr, dt_bias, decay_rate, skip_gain)

    others = [
        by_chips(first, 1),
        by_chips(first, -1),
        by_chips(halves[0], 2),
        by_chips(halves[1], -2),
    ]
    first, xn = lax.optimization_barrier((first, xn))
    weights = jnp.concatenate([first] + others, axis=0)
    sibling = swap(weights)

    pay, kid = kernel(
        project,
        2,
        12,
        (shape(ROWS, 256), shape(24, ROWS, dtype=F32)),
        [SMEM] + [VMEM] * 4,
        [pltpu.VMEM((D, 256), BF)],
    )(scal, xn, weights, sibling, states)
    q = kernel(
        query,
        5,
        52,
        shape(ROWS, COLS),
        [SMEM, VMEM, ANY],
        [
            pltpu.VMEM((D, COLS), BF),
            pltpu.VMEM((ROWS, COLS), F32),
            pltpu.SemaphoreType.DMA((8,)),
        ],
    )(scal, xn, wq)

    back4, back8 = by_chips(pay, 4), by_chips(pay, 8)
    near = jnp.concatenate([pay, back4], axis=0)
    far = jnp.concatenate([back4, back8], axis=0)
    own = jnp.concatenate(
        [pay, back4, back8, by_chips(near, 2), by_chips(near, 1), by_chips(far, -1)], axis=0
    )
    sib = swap(own)
    sib, q = lax.optimization_barrier((sib, q))

    gathered = kernel(
        assemble,
        1,
        16,
        (
            shape(18 * ROWS, HD),
            shape(18 * ROWS, HD),
            shape(ROWS, 18 * ROWS, dtype=F32),
            shape(STATE, COLS, dtype=F32),
            shape(ROWS, ROWS, dtype=F32),
        ),
        [SMEM] + [VMEM] * 5,
    )(scal, own, sib, kid, aux, idc)
    keys, values, mask, incoming, reach = gathered
    made, moved = [], []
    for body, us, cols in ((finish_low, 4, 768), (finish_high, 2, 256)):
        part = kernel(body, us, 20, shape(ROWS, cols), [SMEM] + [VMEM] * 9)(
            scal, hidden_in[0], q, keys, values, mask, yloc, aux, incoming, reach
        )
        made.append(part)
        q, part = lax.optimization_barrier((q, part))
        moved.append(lax.ppermute(part, "pipe", [(i, i + 1) for i in range(3)]))
    produced, moved = jnp.concatenate(made, axis=1), jnp.concatenate(moved, axis=1)
    return (produced[None], moved[None])


def solution(mesh):
    in_specs = (
        P("pipe", "ctx", "tp"),
        P("ctx"),
        P("pipe"),
        P("pipe", "tp"),
        P("pipe", "ctx", "tp"),
        P("pipe", "ctx", "tp"),
        P("pipe", "ctx", "tp"),
        P("pipe", "tp", None),
        P("pipe", "tp", None),
        P("pipe", "tp"),
        P("pipe", "tp"),
        P("pipe", "tp"),
    )
    out_specs = (P("pipe", "ctx", "tp"), P("pipe", "ctx", "tp"))
    return jax.shard_map(shards, mesh=mesh, in_specs=in_specs, out_specs=out_specs, check_vma=False)
```

```python
import jax
import jax.numpy as jnp
from jax import lax
from jax.experimental import pallas as pl
from jax.experimental.pallas import tpu as pltpu
from jax.sharding import PartitionSpec as P

D = 4096
HD = 128
ROWS = 128
COLS = 1024
CHIPS = 16
STATE = 16
HL = 16
WROWS = ROWS + 16
BACK = 8
NEG = -1e30
BF, F32 = jnp.bfloat16, jnp.float32
EXACT = lax.Precision.HIGHEST

W_FIRST = (-4, 0, 4, -8)
W_REL = W_FIRST + (-6, -2, 2, 6) + tuple(a + b for b in (-1, 1) for a in W_FIRST)
KV_AT = (0, 5, 3, 7, 1, 6, 4, 8, 2)


def iota(shape, dim):
    return lax.broadcasted_iota(jnp.int32, shape, dim)


def dot(a, b, precision=None):
    return jnp.dot(a, b, preferred_element_type=F32, precision=precision)


def pair(low, j, values):
    return jnp.where(low, values[:, 2 * j : 2 * j + 1], values[:, 2 * j + 1 : 2 * j + 2])


def front(scal, got, idc_ref, idr_ref, bias, rate, skip, xn, states, yloc, aux):
    attention, place = scal[0], scal[1]
    squares = jnp.zeros((ROWS, 1), F32)
    for s in range(4):
        hf = got[s, :ROWS, :].astype(F32)
        squares += jnp.sum(hf * hf, axis=1, keepdims=True)
    inverse = lax.rsqrt(squares / D + 1e-05)
    for s in range(4):
        gain = got[s, ROWS + 48 :, :].astype(F32)
        gain = gain[0:1] + gain[1:2] + gain[2:3]
        xn[:, s * COLS : (s + 1) * COLS] = (got[s, :ROWS, :].astype(F32) * inverse * gain).astype(BF)
    idc, idr = idc_ref[...], idr_ref[...]

    @pl.when(attention == 0)
    def _():
        maps = jnp.zeros((ROWS, 48), F32)
        for s in range(4):
            maps += lax.dot_general(
                xn[:, s * COLS : (s + 1) * COLS],
                got[s, ROWS : ROWS + 48, :],
                (((1,), (1,)), ((), ())),
                preferred_element_type=F32,
            )
        raw = maps[:, :HL] + bias[...]
        step = jnp.maximum(raw, 0.0) + jnp.log1p(jnp.exp(-jnp.abs(raw)))
        in_map, out_map = maps[:, HL : HL + STATE], maps[:, HL + STATE :]
        earlier = iota((ROWS, ROWS), 0) >= iota((ROWS, ROWS), 1)
        cum = dot(earlier.astype(F32), -step * rate[...], EXACT)
        empty = jnp.zeros((ROWS, ROWS - 32), F32)
        turned = jnp.concatenate([cum, in_map, empty], axis=1).T
        cum_t, in_t = turned[:HL], turned[HL : HL + STATE]
        both = dot(out_map, in_t, EXACT)
        mask = earlier & (idc == idr)
        last = cum[ROWS - 1 :, :]
        end = jnp.where(idc == idr[:, ROWS - 1 :], jnp.exp(last - cum), 0.0)
        low = iota((ROWS, ROWS), 1) < 64
        base = pl.multiple_of(place * COLS, COLS)
        for j in range(HL // 2):
            x = xn[:, pl.ds(base + j * 128, 128)].astype(F32)
            wx = x * pair(low, j, step)
            weights = [
                jnp.exp(jnp.where(mask, cum[:, i : i + 1] - cum_t[i : i + 1, :], NEG)) * both
                for i in (2 * j, 2 * j + 1)
            ]
            split = jnp.concatenate([jnp.where(low, wx, 0.0), jnp.where(low, 0.0, wx)], axis=0)
            inner = dot(jnp.concatenate(weights, axis=1), split, EXACT)
            yloc[:, j * 128 : (j + 1) * 128] = inner + pair(low[:1], j, skip[...]) * x
            state = dot(in_t, wx * pair(low, j, end), EXACT)
            at = 16 * (j // 2)
            states[at : at + 16, 128 * (j % 2) : 128 * (j % 2) + 128] = state.astype(BF)
        wide = jnp.concatenate([last, jnp.zeros((1, 256 - HL), F32)], axis=1)
        first = wide.astype(BF).astype(F32)
        second = (wide - first).astype(BF).astype(F32)
        third = wide - first - second
        row = iota((64, 256), 0)
        extra = jnp.where(row == 0, first, jnp.where(row == 1, second, jnp.where(row == 2, third, 0.0)))
        states[64:, :] = extra.astype(BF)
        aux[...] = jnp.concatenate([cum, out_map, empty], axis=1)


def project(scal, xn, own_a, own_b, sib_a, sib_b, states, pay, kid, weight):
    attention, chip, core = scal[0], scal[2], scal[3]
    n = 0
    for r in range(BACK + 1):
        k = [w % CHIPS for w in W_REL].index(-r % CHIPS)
        for ref in (own_a, sib_a) if k < 8 else (own_b, sib_b):
            at = (k % 8) * WROWS + ROWS
            kid[n : n + 1, :] = ref[at : at + 16, :ROWS].astype(F32)[0:1, :]
            n += 1

    @pl.when(attention == 1)
    def _():
        for n, rel in enumerate(W_REL):
            at = lax.rem(chip + rel + CHIPS, CHIPS) * 256
            own, sib = (own_a, sib_a) if n < 8 else (own_b, sib_b)
            rows = slice(n % 8 * WROWS, n % 8 * WROWS + ROWS)
            weight[pl.ds(pl.multiple_of(at + core * 128, 128), 128), :] = own[rows, :]
            weight[pl.ds(pl.multiple_of(at + (1 - core) * 128, 128), 128), :] = sib[rows, :]
        pay[...] = dot(xn[...], weight[...]).astype(BF)

    @pl.when(attention == 0)
    def _():
        pay[...] = states[...]


def query(scal, xn, wq, out, wbuf, total, sem):
    @pl.when(scal[0] == 1)
    def _():
        parts = [slice(j * 512, (j + 1) * 512) for j in range(8)]
        copies = [
            pltpu.make_async_copy(wq.at[part, :], wbuf.at[part, :], sem.at[j]) for j, part in enumerate(parts)
        ]
        for copy in copies:
            copy.start()
        for j, (copy, part) in enumerate(zip(copies, parts)):
            copy.wait()
            product = dot(xn[:, part], wbuf[part, :])
            total[...] = product if j == 0 else total[...] + product
        out[...] = total[...].astype(BF)


def attend(pairs, h, q, keys, values, mask, out):
    factor = HD ** (-0.5) * 1.4426950408889634
    for j in pairs:
        at = 256 * j
        rows = jnp.concatenate([q[:, at : at + HD], q[:, at + HD : at + 256]], axis=0)
        scores = lax.dot_general(
            rows, keys[...], (((1,), (1,)), ((), ())), preferred_element_type=F32
        )
        parts, dens = [], []
        for i in range(2):
            s = scores[i * ROWS : (i + 1) * ROWS, :] + mask[...]
            p = jnp.exp2((s - jnp.max(s, axis=1, keepdims=True)) * factor)
            dens.append(jnp.sum(p, axis=1, keepdims=True))
            parts.append(p.astype(BF))
        mixed = dot(jnp.concatenate(parts, axis=0), values[...])
        for i in range(2):
            o = (mixed[i * ROWS : (i + 1) * ROWS, :] / dens[i]).astype(BF).astype(F32)
            cols = slice(at + i * HD, at + (i + 1) * HD)
            out[:, at - 256 * pairs[0] + i * HD : at - 256 * pairs[0] + (i + 1) * HD] = (h[:, cols].astype(F32) + o).astype(BF)


def assemble(scal, own, sib, kid, aux, idc_ref, keys, values, mask, incoming, reach):
    idc = idc_ref[...]
    chip, core, device = scal[2], scal[3], scal[4]

    @pl.when(scal[0] == 1)
    def _():
        n = 0
        for r in range(BACK + 1):
            k = KV_AT[r]
            for mine in (True, False):
                ref = own if mine else sib
                rows = slice(n * ROWS, (n + 1) * ROWS)
                keys[rows, :] = ref[k * ROWS : (k + 1) * ROWS, :HD]
                values[rows, :] = ref[k * ROWS : (k + 1) * ROWS, HD:]
                allowed = idc == kid[n : n + 1, :]
                if r == 0 and mine:
                    allowed = allowed & (iota((ROWS, ROWS), 0) >= iota((ROWS, ROWS), 1))
                else:
                    valid = core == 1 if r == 0 else chip >= r
                    allowed = allowed & (jnp.full((ROWS, ROWS), valid.astype(jnp.int32)) == 1)
                mask[:, rows] = jnp.where(allowed, 0.0, NEG)
                n += 1

    @pl.when(scal[0] == 0)
    def _():
        def block(mine, back):
            return own if mine else sib, KV_AT[back] * ROWS, 2 * back + (0 if mine else 1)

        order = []
        for r in range(1, BACK + 1):
            order.append((block(False, r - 1), block(False, r)))
            order.append((block(True, r), None))

        def read(entry, lo, hi):
            (ref, at, _), other = entry
            tile = ref[at + lo : at + hi, :].astype(F32)
            if other is not None:
                ref, at, _ = other
                tile = jnp.where(core == 1, tile, ref[at + lo : at + hi, :].astype(F32))
            return tile

        before = jnp.zeros((1, HL), F32)
        coefs = []
        previous = None
        for k, entry in enumerate(order, 1):
            tails = [kid[e[2] : e[2] + 1, ROWS - 1 :] for e in entry if e is not None]
            tail = tails[0] if len(tails) == 1 else jnp.where(core == 1, tails[0], tails[1])
            tail = jnp.where(device >= k, tail, -1.0)
            if previous is None:
                previous = tail
            fits = (tail == previous) & (tail >= 0.0)
            coefs.append(jnp.where(fits, jnp.exp(before), 0.0))
            extra = read(entry, 64, 80)
            before += extra[0:1, :HL] + extra[1:2, :HL] + extra[2:3, :HL]
        spread = (iota((HL, COLS), 1) // 64 == iota((HL, COLS), 0)).astype(F32)
        coef = dot(jnp.concatenate(coefs, axis=0), spread, EXACT)
        for c in range(4):
            total = jnp.zeros((STATE, 256), F32)
            for k, entry in enumerate(order):
                total += coef[k : k + 1, c * 256 : (c + 1) * 256] * read(entry, 16 * c, 16 * c + 16)
            incoming[:, c * 256 : (c + 1) * 256] = total
        cum = aux[:, :HL]
        wide = jnp.where(idc == previous, jnp.exp(cum), 0.0)
        reach[...] = jnp.concatenate([wide, jnp.zeros((ROWS, ROWS - HL), F32)], axis=1)


def finish_states(pairs, h, yloc, aux, incoming, reach_ref, out):
    out_map, reach = aux[:, HL : HL + STATE], reach_ref[:, :HL]
    low = iota((ROWS, ROWS), 1) < 64
    for n in range(2 * len(pairs)):
        j = 2 * pairs[0] + n
        cols = slice(j * 128, (j + 1) * 128)
        carried = dot(out_map, incoming[:, cols], EXACT) * pair(low, j, reach)
        y = yloc[:, cols] + carried
        y2 = y * y
        one = jnp.sum(jnp.where(low, y2, 0.0), axis=1, keepdims=True)
        two = jnp.sum(jnp.where(low, 0.0, y2), axis=1, keepdims=True)
        scale = lax.rsqrt(jnp.where(low, one, two) / 64 + 1e-05)
        out[:, n * 128 : (n + 1) * 128] = (h[:, cols].astype(F32) + y * scale).astype(BF)


def finish(pairs, scal, h, q, keys, values, mask, yloc, aux, incoming, reach, out):
    @pl.when(scal[0] == 1)
    def _():
        attend(pairs, h, q, keys, values, mask, out)

    @pl.when(scal[0] == 0)
    def _():
        finish_states(pairs, h, yloc, aux, incoming, reach, out)


def finish_low(*refs):
    finish((0, 1, 2), *refs)


def finish_high(*refs):
    finish((3,), *refs)


VMEM = pl.BlockSpec(memory_space=pltpu.VMEM)
SMEM = pl.BlockSpec(memory_space=pltpu.SMEM)
ANY = pl.BlockSpec(memory_space=pl.ANY)


def kernel(body, us, mib, outs, ins, scratch=()):
    return pl.pallas_call(
        body,
        name=body.__name__,
        out_shape=outs,
        in_specs=ins,
        out_specs=jax.tree.map(lambda _: VMEM, outs),
        scratch_shapes=scratch,
        compiler_params=pltpu.CompilerParams(vmem_limit_bytes=mib << 20),
        cost_estimate=pl.CostEstimate(flops=int(us * 1.15e9), bytes_accessed=1 << 20, transcendentals=0),
    )


def shape(*dims, dtype=BF):
    return jax.ShapeDtypeStruct(dims, dtype)


def by_chips(x, k):
    return lax.ppermute(x, "ctx", [(i, (i + 2 * k) % (2 * CHIPS)) for i in range(2 * CHIPS)])


def swap(x):
    return lax.ppermute(x, "ctx", [(i, i ^ 1) for i in range(2 * CHIPS)])


def shards(
    hidden_in,
    doc_ids,
    layer_kind,
    norm_gain,
    q_weight,
    k_weight,
    v_weight,
    bc_weight,
    dt_weight,
    dt_bias,
    decay_rate,
    skip_gain,
):
    device = lax.axis_index("ctx")
    scal = jnp.stack(
        [layer_kind[0], lax.axis_index("tp"), device // 2, device % 2, device]
    ).astype(jnp.int32)
    ids = doc_ids.astype(F32)
    idc, idr = ids[:, None], ids[None, :]

    wq = lax.all_gather(q_weight[0], "ctx", axis=0, tiled=True)

    gain = norm_gain[0]
    gain1 = lax.reduce_precision(gain, 8, 7)
    gain2 = lax.reduce_precision(gain - gain1, 8, 7)
    gain3 = gain - gain1 - gain2
    gains = jnp.concatenate([jnp.stack([gain1, gain2, gain3]), jnp.zeros((13, COLS), F32)]).astype(BF)
    everyone = lambda x: jnp.broadcast_to(x[None], (4,) + x.shape)
    parts = jnp.concatenate(
        [
            everyone(hidden_in[0]),
            dt_weight[0].T.reshape(4, HL, COLS),
            everyone(bc_weight[0].T),
            everyone(gains),
        ],
        axis=1,
    )
    wkv = jnp.concatenate([k_weight[0], v_weight[0]], axis=1)
    wkv = jnp.concatenate([wkv, jnp.pad(idr.astype(BF), ((0, 15), (0, 128)))], axis=0)
    a, b, c = [by_chips(wkv, k) for k in (4, -4, 8)]
    first = jnp.concatenate([a, wkv, b, c], axis=0)
    halves = [jnp.concatenate([a, wkv], axis=0), jnp.concatenate([wkv, b], axis=0)]
    parts, first, halves = lax.optimization_barrier((parts, first, halves))
    got = lax.all_to_all(parts, "tp", 0, 0)
    xn, states, yloc, aux = kernel(
        front,
        4,
        20,
        (shape(ROWS, D), shape(ROWS, 256), shape(ROWS, COLS, dtype=F32), shape(ROWS, 128, dtype=F32)),
        [SMEM] + [VMEM] * 6,
    )(scal, got, idc, idr, dt_bias, decay_rate, skip_gain)

    others = [
        by_chips(halves[0], 2),
        by_chips(halves[1], -2),
        by_chips(first, 1),
        by_chips(first, -1),
    ]
    first, xn = lax.optimization_barrier((first, xn))
    weights = [jnp.concatenate([first] + others[:2], axis=0), jnp.concatenate(others[2:], axis=0)]
    siblings = [swap(x) for x in weights]

    pay, kid = kernel(
        project,
        2,
        12,
        (shape(ROWS, 256), shape(24, ROWS, dtype=F32)),
        [SMEM] + [VMEM] * 6,
        [pltpu.VMEM((D, 256), BF)],
    )(scal, xn, *weights, *siblings, states)
    q = kernel(
        query,
        5,
        52,
        shape(ROWS, COLS),
        [SMEM, VMEM, ANY],
        [
            pltpu.VMEM((D, COLS), BF),
            pltpu.VMEM((ROWS, COLS), F32),
            pltpu.SemaphoreType.DMA((8,)),
        ],
    )(scal, xn, wq)

    back4, back8 = by_chips(pay, 4), by_chips(pay, 8)
    near = jnp.concatenate([pay, back4], axis=0)
    far = jnp.concatenate([back4, back8], axis=0)
    own = jnp.concatenate(
        [pay, back4, back8, by_chips(near, 2), by_chips(near, 1), by_chips(far, -1)], axis=0
    )
    sib = swap(own)
    sib, q = lax.optimization_barrier((sib, q))

    gathered = kernel(
        assemble,
        1,
        16,
        (
            shape(18 * ROWS, HD),
            shape(18 * ROWS, HD),
            shape(ROWS, 18 * ROWS, dtype=F32),
            shape(STATE, COLS, dtype=F32),
            shape(ROWS, ROWS, dtype=F32),
        ),
        [SMEM] + [VMEM] * 5,
    )(scal, own, sib, kid, aux, idc)
    keys, values, mask, incoming, reach = gathered
    made, moved = [], []
    for body, us, cols in ((finish_low, 4, 768), (finish_high, 2, 256)):
        part = kernel(body, us, 20, shape(ROWS, cols), [SMEM] + [VMEM] * 9)(
            scal, hidden_in[0], q, keys, values, mask, yloc, aux, incoming, reach
        )
        made.append(part)
        q, part = lax.optimization_barrier((q, part))
        moved.append(lax.ppermute(part, "pipe", [(i, i + 1) for i in range(3)]))
    produced, moved = jnp.concatenate(made, axis=1), jnp.concatenate(moved, axis=1)
    return (produced[None], moved[None])


def solution(mesh):
    in_specs = (
        P("pipe", "ctx", "tp"),
        P("ctx"),
        P("pipe"),
        P("pipe", "tp"),
        P("pipe", "ctx", "tp"),
        P("pipe", "ctx", "tp"),
        P("pipe", "ctx", "tp"),
        P("pipe", "tp", None),
        P("pipe", "tp", None),
        P("pipe", "tp"),
        P("pipe", "tp"),
        P("pipe", "tp"),
    )
    out_specs = (P("pipe", "ctx", "tp"), P("pipe", "ctx", "tp"))
    return jax.shard_map(shards, mesh=mesh, in_specs=in_specs, out_specs=out_specs, check_vma=False)
```
